32 devices in a mesh: groups: 2 (over x), src: 16 (over z, y, core).
Axes of the slice: x: 2, y: 2, z: 4, core: 2. Of those that a mesh axis runs over, the one named last changes fastest.
Arguments:
- kernel_band: float32 [2048, 131072], P('groups', 'src'), parts along dimension 0, may hold values from -0.0234375 to 0.0234375
- slip_field: float32 [1024, 131072], P(('groups', 'src')), parts along dimension 0, may hold values from -6 to 6
- elements: int32 [2048], P('groups'), parts along dimension 0, may hold values from 0 to 131071, as said below
- classes: int32 [2048, 512], P(('groups', 'src')), parts along dimension 0, may hold values from 0 to 7
- shear_load: float32 [2048], P(('groups', 'src')), parts along dimension 0, may hold values from 0.5 to 1.5
- normal_stress: float32 [2048], P(('groups', 'src')), parts along dimension 0, may hold values from 0.5 to 2
- static_friction: float32 [8], replicated, may hold values from 0.6 to 0.9
- dynamic_friction: float32 [8], replicated, may hold values from 0.1 to 0.5
- weakening_slip: float32 [8], replicated, may hold values from 0.3 to 3
Outputs:
- shear_stress: float32 [2048, 512], P(('groups', 'src')), parts along dimension 0
- slip_rate: float32 [2048, 512], P(('groups', 'src')), parts along dimension 0
The draws below stay inside these ranges and needn't reach their ends.
There are 2 independent parts, one for each index of `groups`. The reference program is written for one: setup_inputs(seed, part) draws one part's arguments, and reference() takes and returns one part's arrays. A program takes and returns all parts, laid end to end along the dimension named above; an argument that names none is the same for every part. Nothing has to cross between parts.
Inputs may be any that keep to these rules, and one draw needn't show every extreme that they name: `elements`: the 1024 element numbers are distinct.
All inputs are finite; a program needn't handle non-finite values.
Results may differ from the reference program's by a relative error of at most 0.000059.
Values sent between devices are 32-bit elements; how exact they have to be, the bound alone decides.
No kernel may reach another device: no remote copies, remote signals or barrier semaphores. Data moves between devices by JAX's collectives and lax.ppermute only.
A program may use at most 192 MiB of HBM per device.

```python
import math
import jax
import jax.numpy as jnp
from jax import lax

N = 131072
R = 1024
M = 512
NCLASS = 8


def draw_elements(key, part):
    key = jax.random.fold_in(key, 7)
    first_key, second_key = jax.random.split(key)
    inner = jax.random.permutation(first_key, N - 2)[:R - 2].astype(jnp.int32) + 1
    values = jnp.concatenate([jnp.array([0, N - 1], jnp.int32), inner])
    order = jax.random.permutation(second_key, R)
    return values[order]


def plant(drawn, key, smallest, high):
    longest = drawn.shape.index(max(drawn.shape))
    spots = []
    for shift in (0, 1):
        where = [jax.random.randint(jax.random.fold_in(key, axis), (), 0, length) for axis, length in enumerate(drawn.shape)]
        where[longest] = (where[longest] + shift) % drawn.shape[longest]
        spots.append(tuple(where))
    return drawn.at[spots[0]].set(smallest).at[spots[1]].set(high)


def strengthened(entries, rng, source, target, shards_of, factor):
    def block_of(position):
        return (jnp.arange(entries.shape[position]) // (entries.shape[position] // shards_of)).reshape((-1,) + (1,) * (entries.ndim - 1 - position))

    one_side = jax.random.permutation(rng, shards_of)[block_of(target)]
    second = (block_of(target) + shards_of // 2) % shards_of
    return jnp.where((block_of(source) == one_side) | (block_of(source) == second), factor * entries, entries)


def block_levels(key, dims, cuts, smallest, top_value):
    factor_of = 1.0
    for position, blocks in cuts:
        steps = jax.random.uniform(jax.random.fold_in(jax.random.fold_in(key, 6), position), (blocks,), jnp.float32, smallest / len(cuts), top_value / len(cuts))
        factor_of = factor_of * jnp.repeat(jnp.exp(steps), dims[position] // blocks).reshape((-1,) + (1,) * (len(dims) - 1 - position))
    return factor_of


def gaussian(own_key, extent, width, limit, cuts=(), kind=jnp.bfloat16):
    entries = jax.random.normal(own_key, extent, jnp.float32) * width
    if len(cuts) > 0:
        entries = block_levels(own_key, extent, cuts, -0.22, 0.18) * entries
    return jnp.clip(entries, min=-limit, max=limit).astype(kind)


def heavy_noise(stream_key, dims, scale, limit, shards, heavy, kind=jnp.bfloat16):
    values = scale * jax.random.normal(stream_key, dims, jnp.float32)
    if shards:
        values = values * block_levels(stream_key, dims, shards, -0.22, 0.18)
    return jnp.clip(strengthened(values, jax.random.fold_in(stream_key, 3), *heavy), -limit, limit).astype(kind)


def setup_inputs(seed: int = 0, part: int = 0) -> dict:
    seeds = jax.random.split(jax.random.key(seed), 10)
    part_keys = jax.random.split(jax.random.fold_in(seeds[9], part), 10)
    kernel_band = heavy_noise(part_keys[0], (R, N), N ** -0.5, 0.0234375, ((1, 16),), (1, 0, 16, 2.0), jnp.float32)
    slip_field = gaussian(part_keys[1], (M, N), 1.0, 6.0, ((0, 16),), jnp.float32)
    elements = draw_elements(jax.random.fold_in(jax.random.fold_in(seeds[9], part), 71), part)
    classes = plant(jax.random.randint(part_keys[3], (R, M), 0, NCLASS), jax.random.fold_in(part_keys[3], 1), 0, NCLASS - 1).astype(jnp.int32)
    shear_load = jnp.clip(0.5 + 1.0 * jax.random.uniform(part_keys[4], (R,), jnp.float32) ** block_levels(part_keys[4], (R,), ((0, 16),), -0.2, 0.2), 0.5, 1.5)
    normal_stress = jnp.clip(jnp.exp(math.log(2.0) - 1.3862944 * jax.random.uniform(part_keys[5], (R,), jnp.float32) ** block_levels(part_keys[5], (R,), ((0, 16),), -0.2, 0.2)), 0.5, 2.0)
    static_friction = jnp.clip(jax.random.uniform(seeds[6], (NCLASS,), jnp.float32, 0.6, 0.9), 0.6, 0.9)
    dynamic_friction = jnp.clip(jax.random.uniform(seeds[7], (NCLASS,), jnp.float32, 0.1, 0.5), 0.1, 0.5)
    weakening_slip = jnp.clip(jnp.exp(jax.random.uniform(seeds[8], (NCLASS,), jnp.float32, math.log(0.3), math.log(3.0))), 0.3, 3.0)
    return {"kernel_band": kernel_band, "slip_field": slip_field, "elements": elements, "classes": classes, "shear_load": shear_load, "normal_stress": normal_stress, "static_friction": static_friction, "dynamic_friction": dynamic_friction, "weakening_slip": weakening_slip}


def lookup(table, classes):
    total = jnp.zeros(classes.shape, jnp.float32)
    for index in range(NCLASS):
        total = total + jnp.where(classes == index, table[index], jnp.float32(0.0))
    return total


def reference(kernel_band, slip_field, elements, classes, shear_load, normal_stress, static_friction, dynamic_friction, weakening_slip):
    traction = jnp.dot(kernel_band, slip_field.T, precision=lax.Precision.HIGHEST, preferred_element_type=jnp.float32)
    shear_stress = shear_load[:, None] + traction
    receiver_slip = jnp.take(slip_field, elements.astype(jnp.int32), axis=1).T
    mu_static = lookup(static_friction, classes)
    mu_dynamic = lookup(dynamic_friction, classes)
    slip_scale = lookup(weakening_slip, classes)
    weakening = jnp.maximum(1.0 - jnp.abs(receiver_slip) / slip_scale, 0.0)
    strength = normal_stress[:, None] * (mu_dynamic + (mu_static - mu_dynamic) * weakening)
    slip_rate = jax.nn.softplus((shear_stress - strength) / 0.25)
    return shear_stress, slip_rate
```

```python
import functools

import jax
import jax.numpy as jnp
from jax import lax
from jax.experimental import pallas as pl
from jax.experimental.pallas import tpu as pltpu
from jax.sharding import PartitionSpec as P

VMEM_LIMIT = 40 * 1024 * 1024
TAIL_ROWS = 8


def halves(x):
    high = x.astype(jnp.bfloat16)
    low = (x - high.astype(jnp.float32)).astype(jnp.bfloat16)
    return high, low


def product_kernel(band_ref, slip_ref, out_ref):
    @pl.when(pl.program_id(0) == 0)
    def _():
        out_ref[...] = jnp.zeros_like(out_ref)

    members = slip_ref.shape[0]
    band_high, band_low = halves(band_ref[...])
    slip_high, slip_low = halves(slip_ref[...])
    over_last = (((1,), (1,)), ((), ()))
    wide = lax.dot_general(
        band_high,
        jnp.concatenate([slip_high, slip_low], axis=0),
        over_last,
        preferred_element_type=jnp.float32,
    )
    narrow = lax.dot_general(band_low, slip_high, over_last, preferred_element_type=jnp.float32)
    out_ref[...] += wide[:, :members] + (wide[:, members:] + narrow)


def product(band, slip, tile=512):
    rows, depth = band.shape
    members = slip.shape[0]
    return pl.pallas_call(
        product_kernel,
        grid=(depth // tile,),
        in_specs=[
            pl.BlockSpec((rows, tile), lambda i: (0, i)),
            pl.BlockSpec((members, tile), lambda i: (0, i)),
        ],
        out_specs=pl.BlockSpec((rows, members), lambda i: (0, 0)),
        out_shape=jax.ShapeDtypeStruct((rows, members), jnp.float32),
        compiler_params=pltpu.CompilerParams(vmem_limit_bytes=VMEM_LIMIT),
        cost_estimate=pl.CostEstimate(
            flops=6 * rows * depth * members,
            bytes_accessed=4 * (rows * depth + members * depth + rows * members),
            transcendentals=0,
        ),
        name="stress_product",
    )(band, slip)


def swap(x, bit, ways):
    return lax.ppermute(x, "src", [(i, i ^ bit) for i in range(ways)])


def owner_sums(partial, me, ways):
    columns = partial.shape[1]
    own = partial.shape[0] // ways
    left, bit = partial, 1
    while bit < ways:
        pairs = left.reshape(ways // bit // 2, 2, own, columns)
        mine = (me // bit) & 1
        kept = lax.dynamic_index_in_dim(pairs, mine, 1, keepdims=False)
        given = lax.dynamic_index_in_dim(pairs, 1 - mine, 1, keepdims=False)
        left = kept + swap(given, bit, ways)
        bit *= 2
    return left.reshape(own, columns)


def friction_kernel(
    static_ref, dynamic_ref, scale_ref, first_ref, last_ref, spread_ref, slip_ref, classes_ref, load_ref, normal_ref, stress_ref, rate_ref
):
    total = first_ref[...] + lax.dot_general(
        last_ref[...],
        spread_ref[...],
        (((1,), (0,)), ((), ())),
        precision=lax.Precision.HIGHEST,
        preferred_element_type=jnp.float32,
    )
    stress = load_ref[...] + total
    classes = classes_ref[...]
    zero = jnp.zeros(classes.shape, jnp.float32)
    mu_static, mu_dynamic, slip_scale = zero, zero, zero
    for index in range(static_ref.shape[0]):
        here = classes == index
        mu_static = jnp.where(here, static_ref[index], mu_static)
        mu_dynamic = jnp.where(here, dynamic_ref[index], mu_dynamic)
        slip_scale = jnp.where(here, scale_ref[index], slip_scale)
    weakening = jnp.maximum(1.0 - jnp.abs(slip_ref[...]) / slip_scale, 0.0)
    strength = normal_ref[...] * (mu_dynamic + (mu_static - mu_dynamic) * weakening)
    excess = (stress - strength) / 0.25
    stress_ref[...] = stress
    rate_ref[...] = jnp.maximum(excess, 0.0) + jnp.log1p(jnp.exp(-jnp.abs(excess)))


def friction(first, last, spread, slip, classes, load, normal, static, dynamic, scale):
    table = pl.BlockSpec(memory_space=pltpu.SMEM)
    whole = pl.BlockSpec(memory_space=pltpu.VMEM)
    shape = jax.ShapeDtypeStruct(classes.shape, jnp.float32)
    return pl.pallas_call(
        friction_kernel,
        in_specs=[table] * 3 + [whole] * 7,
        out_specs=[whole] * 2,
        out_shape=[shape, shape],
        name="friction",
    )(static, dynamic, scale, first, last, spread, slip, classes, load[:, None], normal[:, None])


def shards(
    ways,
    kernel_band,
    slip_field,
    elements,
    classes,
    shear_load,
    normal_stress,
    static_friction,
    dynamic_friction,
    weakening_slip,
):
    me = lax.axis_index("src")
    members, total_elements = slip_field.shape
    depth = total_elements // ways
    own = classes.shape[0]
    tail = min(TAIL_ROWS, members)
    head = members - tail

    def to_blocks(rows):
        return jnp.swapaxes(rows.reshape(rows.shape[0], ways, depth), 0, 1)

    at_receivers = jnp.take(slip_field, elements, axis=1)
    riders = at_receivers.reshape(members // tail, tail, ways, own)
    riders = riders.transpose(2, 1, 0, 3).reshape(ways, tail, -1)

    sums = []
    if head:
        first = lax.all_to_all(to_blocks(slip_field[:head]), "src", 0, 0, tiled=True)
        sums.append((head, product(kernel_band, first.reshape(ways * head, depth))))
    payload = jnp.concatenate([to_blocks(slip_field[head:]), riders], axis=2)
    last = lax.all_to_all(payload, "src", 0, 0, tiled=True)
    last_product = product(kernel_band, last.reshape(ways * tail, -1))
    receiver_slip = last[:, :, depth:].reshape(ways, tail, members // tail, own)
    receiver_slip = receiver_slip.transpose(3, 0, 2, 1).reshape(own, ways * members)

    if head:
        first_sums = owner_sums(sums[0][1], me, ways).reshape(own, ways, head)
        first_sums = jnp.pad(first_sums, ((0, 0), (0, 0), (0, tail))).reshape(own, ways * members)
    else:
        first_sums = jnp.zeros((own, ways * members), jnp.float32)
    last_sums = owner_sums(last_product, me, ways)
    place = lax.broadcasted_iota(jnp.int32, (ways * tail, ways * members), 1)
    source = lax.broadcasted_iota(jnp.int32, (ways * tail, ways * members), 0)
    spread = (place == source // tail * members + head + source % tail).astype(jnp.float32)
    return friction(
        first_sums,
        last_sums,
        spread,
        receiver_slip,
        classes,
        shear_load,
        normal_stress,
        static_friction,
        dynamic_friction,
        weakening_slip,
    )


def solution(mesh):
    placed = (
        P("groups", "src"),
        P(("groups", "src"), None),
        P("groups"),
        P(("groups", "src"), None),
        P(("groups", "src")),
        P(("groups", "src")),
        P(),
        P(),
        P(),
    )
    return jax.shard_map(
        functools.partial(shards, mesh.shape["src"]),
        mesh=mesh,
        in_specs=placed,
        out_specs=(P(("groups", "src"), None), P(("groups", "src"), None)),
        check_vma=False,
    )
```

```python
import functools

import jax
import jax.numpy as jnp
from jax import lax
from jax.experimental import pallas as pl
from jax.experimental.pallas import tpu as pltpu
from jax.sharding import PartitionSpec as P

VMEM_LIMIT = 48 * 1024 * 1024
TAIL_ROWS = 8
IN_FLIGHT = 4
TILE = 2048
FIRST_WEIGHT = 10
LANES = 128
ANY = pl.BlockSpec(memory_space=pl.ANY)
AFTER = pl.BlockSpec(memory_space=pltpu.HBM)
SCALARS = pl.BlockSpec(memory_space=pltpu.SMEM)
WHOLE = pl.BlockSpec(memory_space=pltpu.VMEM)
OVER_LAST = (((1,), (1,)), ((), ()))


def halves(x):
    high = x.astype(jnp.bfloat16)
    low = (x - high.astype(jnp.float32)).astype(jnp.bfloat16)
    return high, low


def split_kernel(band_ref, after_ref, out_ref):
    del after_ref
    tile = band_ref.shape[1]
    out_ref[:, pl.ds(0, tile)], out_ref[:, pl.ds(tile, tile)] = halves(band_ref[...])


def split(band, after):
    receivers, depth = band.shape
    tile, rows = min(TILE, depth), receivers // 4
    return pl.pallas_call(
        split_kernel,
        grid=(4, depth // tile),
        in_specs=[pl.BlockSpec((rows, tile), lambda i, j: (i, j)), AFTER],
        out_specs=pl.BlockSpec((rows, 2 * tile), lambda i, j: (i, j)),
        out_shape=jax.ShapeDtypeStruct((receivers, 2 * depth), jnp.bfloat16),
        compiler_params=pltpu.CompilerParams(vmem_limit_bytes=VMEM_LIMIT),
        cost_estimate=pl.CostEstimate(flops=0, bytes_accessed=8 * receivers * depth, transcendentals=0),
        name="band_halves",
    )(band, after)


def multiply(band_ref, slip):
    members = slip.shape[0]
    high, low = halves(slip)
    both = jnp.concatenate([high, low], axis=0)
    mixed = lax.dot_general(
        band_ref[...], jnp.concatenate([both, both], axis=1), OVER_LAST, preferred_element_type=jnp.float32
    )
    return mixed[:, :members] + mixed[:, members:]


def accumulate(total_scr, band_ref, slip):
    step = pl.program_id(0)
    now = multiply(band_ref, slip)

    @pl.when(step == 0)
    def _():
        total_scr[...] = now

    @pl.when(step > 0)
    def _():
        total_scr[...] += now


def in_order(me_ref, ks, slip_refs, slip_scr):
    rows = slip_refs[0].shape[0]
    for k, ref in zip(ks, slip_refs):
        place = pl.multiple_of(((me_ref[0] ^ k) >> 1) * rows, 8)
        slip_scr[pl.ds(place, rows), :] = ref[...]
    return slip_scr[...]


def like_product_kernel(ks, me_ref, band_ref, *refs):
    slip_refs, (after_ref, out_ref, slip_scr) = refs[: len(ks)], refs[len(ks) :]
    del after_ref
    accumulate(out_ref, band_ref, in_order(me_ref, ks, slip_refs, slip_scr))


def part_rows(me_ref, kept_ref, given_ref, parts, crossed):
    pairs, own, _ = kept_ref.shape
    mine = me_ref[0] & 1
    for pair in range(pairs):
        for out_ref, order, parity in ((kept_ref, parts, mine), (given_ref, crossed, 1 - mine)):
            rows = pl.ds(pl.multiple_of((2 * pair + parity) * own, 8), own)
            out_ref[pair] = jnp.concatenate([ref[rows, :] for ref in order], axis=1)


def unlike_product_kernel(ks, me_ref, band_ref, *refs):
    slip_refs, (like_ref, kept_ref, given_ref, slip_scr, total_scr) = refs[: len(ks)], refs[len(ks) :]
    accumulate(total_scr, band_ref, in_order(me_ref, ks, slip_refs, slip_scr))

    @pl.when(pl.program_id(0) == pl.num_programs(0) - 1)
    def _():
        part_rows(me_ref, kept_ref, given_ref, (like_ref, total_scr), (total_scr, like_ref))


def last_product_kernel(me_ref, band_ref, slip_ref, after_ref, kept_ref, given_ref, total_scr):
    del after_ref
    accumulate(total_scr, band_ref, slip_ref[...])

    @pl.when(pl.program_id(0) == pl.num_programs(0) - 1)
    def _():
        part_rows(me_ref, kept_ref, given_ref, (total_scr,), (total_scr,))


def product(kernel, name, me, band, slip, slip_specs, extra, extra_spec, members, ways, scratch, weight, columns=None):
    receivers, depth = band.shape[0], band.shape[1] // 2
    tile = min(TILE, depth)
    if columns is None:
        shape, many = (receivers, members), 1
    else:
        shape, many = (ways // 2, receivers // ways, columns), 2
    out = pl.BlockSpec(shape, lambda i, me_ref: (0,) * len(shape))
    outs = pl.pallas_call(
        kernel,
        grid_spec=pltpu.PrefetchScalarGridSpec(
            num_scalar_prefetch=1,
            grid=(depth // tile,),
            in_specs=[pl.BlockSpec((receivers, 2 * tile), lambda i, me_ref: (0, i)), *slip_specs, extra_spec],
            out_specs=[out] * many,
            scratch_shapes=[pltpu.VMEM(rows_columns, jnp.float32) for rows_columns in scratch],
        ),
        out_shape=[jax.ShapeDtypeStruct(shape, jnp.float32)] * many,
        compiler_params=pltpu.CompilerParams(vmem_limit_bytes=VMEM_LIMIT),
        cost_estimate=pl.CostEstimate(
            flops=weight * 8 * receivers * depth * members,
            bytes_accessed=4 * (receivers * depth + members * depth),
            transcendentals=0,
        ),
        name=name,
    )(me, band, *slip, extra)
    return outs if many == 2 else outs[0]


def first_products(me, band, slip_field, got, ways, after):
    receivers, depth = band.shape[0], band.shape[1] // 2
    tile = min(TILE, depth)
    rows = got[2].shape[0]
    members, steps = ways // 2 * rows, depth // tile
    mine = pl.BlockSpec((rows, tile), lambda i, me_ref: (0, me_ref[0] * steps + i))
    block = pl.BlockSpec((rows, tile), lambda i, me_ref: (0, i))
    even, odd = list(range(0, ways, 2)), list(range(1, ways, 2))
    like = product(
        functools.partial(like_product_kernel, even), "like_product", me, band,
        [slip_field] + [got[k] for k in even[1:]], [mine] + [block] * (len(even) - 1), after, AFTER,
        members, ways, [(members, tile)], 1,
    )
    whole = pl.BlockSpec((receivers, members), lambda i, me_ref: (0, 0))
    return like, lambda: product(
        functools.partial(unlike_product_kernel, odd), "unlike_product", me, band,
        [got[k] for k in odd], [block] * len(odd), like, whole,
        members, ways, [(members, tile), (receivers, members)], FIRST_WEIGHT, 2 * members,
    )


def last_product(me, band, slip, after, ways):
    receivers, depth = band.shape[0], band.shape[1] // 2
    members = slip.shape[0]
    spec = pl.BlockSpec((members, min(TILE, depth)), lambda i, me_ref: (0, i))
    return product(
        last_product_kernel, "last_product", me, band, [slip], [spec], after, AFTER,
        members, ways, [(receivers, members)], 1, members,
    )


def fold_kernel(me_ref, kept_ref, came_ref, *out_refs):
    for k, out_ref in enumerate(out_refs):
        pair = (me_ref[0] >> 1) ^ k
        out_ref[...] = kept_ref[pair] + came_ref[pair]


def last_sums(me, kept, given, ways):
    pairs = ways // 2
    shape = jax.ShapeDtypeStruct(kept.shape[1:], jnp.float32)
    blocks = pl.pallas_call(
        fold_kernel,
        in_specs=[SCALARS, WHOLE, WHOLE],
        out_specs=[WHOLE] * pairs,
        out_shape=[shape] * pairs,
        name="pair_sums",
    )(me, kept, swap(given, 1, ways))
    return [blocks[0]] + [swap(blocks[k], 2 * k, ways) for k in range(1, pairs)]


def pack_kernel(to_ref, slip_ref, *refs):
    del to_ref
    out_ref = refs[-1]
    out_ref[...] = slip_ref[...]


def pack(to, slip_field, rows, depth, after):
    return pl.pallas_call(
        pack_kernel,
        grid_spec=pltpu.PrefetchScalarGridSpec(
            num_scalar_prefetch=1,
            grid=(1,),
            in_specs=[pl.BlockSpec((rows, depth), lambda i, to_ref: (0, to_ref[0]))] + [AFTER] * len(after),
            out_specs=pl.BlockSpec((rows, depth), lambda i, to_ref: (0, 0)),
        ),
        out_shape=jax.ShapeDtypeStruct((rows, depth), jnp.float32),
        cost_estimate=pl.CostEstimate(flops=0, bytes_accessed=8 * rows * depth, transcendentals=0),
        name="pack_block",
    )(to, slip_field, *after)


def pack_all_kernel(slip_ref, riders_ref, *refs):
    out_ref = refs[-1]
    depth = slip_ref.shape[1]
    out_ref[0, :, pl.ds(0, depth)] = slip_ref[...]
    out_ref[0, :, pl.ds(depth, riders_ref.shape[2])] = riders_ref[0]


def pack_all(slip_field, start, rows, riders, after):
    ways, _, width = riders.shape
    depth = slip_field.shape[1] // ways
    return pl.pallas_call(
        pack_all_kernel,
        grid=(ways,),
        in_specs=[
            pl.BlockSpec((rows, depth), lambda i: (start // rows, i)),
            pl.BlockSpec((1, rows, width), lambda i: (i, 0, 0)),
        ]
        + [AFTER] * len(after),
        out_specs=pl.BlockSpec((1, rows, depth + width), lambda i: (i, 0, 0)),
        out_shape=jax.ShapeDtypeStruct((ways, rows, depth + width), jnp.float32),
        cost_estimate=pl.CostEstimate(flops=0, bytes_accessed=8 * ways * rows * (depth + width), transcendentals=0),
        name="pack_all",
    )(slip_field, riders, *after)


def gather_kernel(elements_ref, slip_ref, after_ref, out_ref, tiles, sems):
    del after_ref
    groups = out_ref.shape[1] // LANES

    def fetch(g):
        def one(j, carry):
            first = pl.multiple_of((elements_ref[g * LANES + j] >> 7) << 7, LANES)
            pltpu.make_async_copy(slip_ref.at[:, pl.ds(first, LANES)], tiles.at[g & 1, j], sems.at[g & 1]).start()
            return carry

        lax.fori_loop(0, LANES, one, 0, unroll=8)

    lanes = lax.broadcasted_iota(jnp.int32, tiles.shape[2:], 1)
    fetch(0)
    for g in range(groups):
        if g + 1 < groups:
            fetch(g + 1)
        slot = tiles.at[g & 1]
        pltpu.make_async_copy(slot, slot, sems.at[g & 1]).wait()

        def one(j, found, g=g, slot=slot):
            shift = (j - elements_ref[g * LANES + j]) & (LANES - 1)
            return jnp.where(lanes == j, pltpu.roll(slot[j], shift, axis=1), found)

        found = lax.fori_loop(0, LANES, one, jnp.zeros(tiles.shape[2:], jnp.float32), unroll=16)
        out_ref[:, pl.ds(g * LANES, LANES)] = found


def gather(elements, slip_field, after):
    members, count = slip_field.shape[0], elements.shape[0]
    return pl.pallas_call(
        gather_kernel,
        in_specs=[SCALARS, ANY, AFTER],
        out_specs=WHOLE,
        out_shape=jax.ShapeDtypeStruct((members, count), jnp.float32),
        scratch_shapes=[pltpu.VMEM((2, LANES, members, LANES), jnp.float32), pltpu.SemaphoreType.DMA((2,))],
        cost_estimate=pl.CostEstimate(flops=0, bytes_accessed=4 * members * LANES * count, transcendentals=0),
        name="slip_at_receivers",
    )(elements, slip_field, after)


def swap(x, bit, ways):
    return lax.ppermute(x, "src", [(i, i ^ bit) for i in range(ways)])


def owner_sums(kept, given, me, ways):
    _, own, columns = kept.shape
    bit = 1
    while True:
        came = swap(given, bit, ways)
        bit *= 2
        if bit >= ways:
            return [kept.reshape(own, columns), came.reshape(own, columns)], given
        pairs = (kept + came).reshape(ways // bit // 2, 2, own, columns)
        mine = (me // bit) & 1
        kept = lax.dynamic_index_in_dim(pairs, mine, 1, keepdims=False)
        given = lax.dynamic_index_in_dim(pairs, 1 - mine, 1, keepdims=False)


def spread(x, columns, place):
    shape = (x.shape[1], columns)
    wanted = place(lax.broadcasted_iota(jnp.int32, shape, 0))
    chosen = jnp.where(lax.broadcasted_iota(jnp.int32, shape, 1) == wanted, 1.0, 0.0).astype(jnp.float32)
    return lax.dot_general(
        x, chosen, (((1,), (0,)), ((), ())), precision=lax.Precision.HIGHEST, preferred_element_type=jnp.float32
    )


def upright(row):
    shape = (row.shape[1], row.shape[1])
    diagonal = lax.broadcasted_iota(jnp.int32, shape, 0) == lax.broadcasted_iota(jnp.int32, shape, 1)
    return jnp.sum(jnp.where(diagonal, row, 0.0), axis=1, keepdims=True)


def strength_kernel(static_ref, dynamic_ref, scale_ref, riders_ref, classes_ref, normal_ref, after_ref, out_ref):
    del after_ref
    ways, tail, width = riders_ref.shape
    own, columns = classes_ref.shape
    members = columns // ways
    turned = riders_ref[...].reshape(ways * tail, width).T
    groups = [turned[g * own : (g + 1) * own] for g in range(members // tail)]
    count = ways * tail
    slip = spread(
        jnp.concatenate(groups, axis=1),
        columns,
        lambda j: j % count // tail * members + j // count * tail + j % tail,
    )
    classes = classes_ref[...]
    zero = jnp.zeros(classes.shape, jnp.float32)
    mu_static, mu_dynamic, slip_scale = zero, zero, zero
    for index in range(static_ref.shape[0]):
        here = classes == index
        mu_static = jnp.where(here, static_ref[index], mu_static)
        mu_dynamic = jnp.where(here, dynamic_ref[index], mu_dynamic)
        slip_scale = jnp.where(here, scale_ref[index], slip_scale)
    weakening = jnp.maximum(1.0 - jnp.abs(slip) / slip_scale, 0.0)
    out_ref[...] = upright(normal_ref[...]) * (mu_dynamic + (mu_static - mu_dynamic) * weakening)


def strength(last, width, classes, normal, static, dynamic, scale, after):
    ways, tail, total = last.shape
    return pl.pallas_call(
        strength_kernel,
        grid=(1,),
        in_specs=[SCALARS] * 3
        + [pl.BlockSpec((ways, tail, width), lambda i: (0, 0, total // width - 1))]
        + [pl.BlockSpec(classes.shape, lambda i: (0, 0)), pl.BlockSpec((1, normal.shape[0]), lambda i: (0, 0)), AFTER],
        out_specs=pl.BlockSpec(classes.shape, lambda i: (0, 0)),
        out_shape=jax.ShapeDtypeStruct(classes.shape, jnp.float32),
        name="strength",
    )(static, dynamic, scale, last, classes, normal[None, :], after)


def slip_rate_kernel(ways, n_first, me_ref, load_ref, strength_ref, *refs):
    *term_refs, stress_ref, rate_ref = refs
    columns = stress_ref.shape[1]
    members = columns // ways
    last = sum(ref[...] for ref in term_refs[n_first:])
    tail = last.shape[1] // ways
    head = members - tail
    total = spread(last, columns, lambda j: j // tail * members + head + j % tail)
    if n_first:
        first = sum(ref[...] for ref in term_refs[:n_first])
        half = ways // 2 * head
        parity = me_ref[0] & 1
        total = total + spread(
            first,
            columns,
            lambda j: (j % half // head * 2 + (j // half ^ parity)) * members + j % half % head,
        )
    stress = upright(load_ref[...]) + total
    excess = (stress - strength_ref[...]) / 0.25
    stress_ref[...] = stress
    rate_ref[...] = jnp.maximum(excess, 0.0) + jnp.log1p(jnp.exp(-jnp.abs(excess)))


def slip_rate(ways, me, load, strong, first, last):
    terms = [*first, *last]
    shape = jax.ShapeDtypeStruct(strong.shape, jnp.float32)
    return pl.pallas_call(
        functools.partial(slip_rate_kernel, ways, len(first)),
        in_specs=[SCALARS] + [WHOLE] * (2 + len(terms)),
        out_specs=[WHOLE] * 2,
        out_shape=[shape, shape],
        name="slip_rate",
    )(me, load[None, :], strong, *terms)


def partners(ways):
    half, quarter = ways // 2, ways // 4
    order = []
    for parity in (0, 1):
        near = [k for k in [*range(quarter, half), *range(1, quarter)] if k % 2 == parity]
        for far in range(half + parity, ways, 2):
            order.append(far)
            if near:
                order.append(near.pop(0))
    return order


def shards(
    ways,
    kernel_band,
    slip_field,
    elements,
    classes,
    shear_load,
    normal_stress,
    static_friction,
    dynamic_friction,
    weakening_slip,
):
    me = lax.axis_index("src").astype(jnp.int32)
    here = me.reshape(1)
    members, total_elements = slip_field.shape
    depth = total_elements // ways
    own = classes.shape[0]
    tail = min(TAIL_ROWS, members)
    head = members - tail

    came, got, block = [slip_field] * IN_FLIGHT, {}, slip_field
    if head:
        for turn, k in enumerate(partners(ways)):
            block = pack(here ^ k, slip_field, head, depth, (came[-IN_FLIGHT], block))
            got[k] = swap(block, k, ways)
            came.append(got[k])
            if turn == 2:
                came[-1] = at_receivers = gather(elements, slip_field, came[-1])
            if turn == 4:
                came[-1] = band = split(kernel_band, came[-1])
            if turn == 7:
                came[-1], unlike = first_products(here, band, slip_field, got, ways, came[-1])
    else:
        at_receivers = gather(elements, slip_field, slip_field)
        band = split(kernel_band, slip_field)

    riders = at_receivers.reshape(members // tail, tail, ways, own)
    riders = riders.transpose(2, 1, 0, 3).reshape(ways, tail, -1)
    riders = jnp.pad(riders, ((0, 0), (0, 0), (0, -riders.shape[2] % LANES)))
    last = lax.all_to_all(pack_all(slip_field, head, tail, riders, (came[-IN_FLIGHT], block)), "src", 0, 0, tiled=True)

    first_terms, after = [], slip_field
    if head:
        first_terms, after = owner_sums(*unlike(), me, ways)
    kept, given = last_product(here, band, last.reshape(ways * tail, -1), after, ways)
    strong = strength(
        last, riders.shape[2], classes, normal_stress, static_friction, dynamic_friction, weakening_slip, given
    )
    return slip_rate(ways, here, shear_load, strong, first_terms, last_sums(here, kept, given, ways))


def solution(mesh):
    placed = (
        P("groups", "src"),
        P(("groups", "src"), None),
        P("groups"),
        P(("groups", "src"), None),
        P(("groups", "src")),
        P(("groups", "src")),
        P(),
        P(),
        P(),
    )
    return jax.shard_map(
        functools.partial(shards, mesh.shape["src"]),
        mesh=mesh,
        in_specs=placed,
        out_specs=(P(("groups", "src"), None), P(("groups", "src"), None)),
        check_vma=False,
    )
```

```python
import functools

import jax
import jax.numpy as jnp
from jax import lax
from jax.experimental import pallas as pl
from jax.experimental.pallas import tpu as pltpu
from jax.sharding import PartitionSpec as P

VMEM_LIMIT = 48 * 1024 * 1024
SMALL = pltpu.CompilerParams(vmem_limit_bytes=8 * 1024 * 1024)
TAIL_ROWS = 8
IN_FLIGHT = 4
TILE = 2048
FIRST_WEIGHT = 10
LANES = 128
ANY = pl.BlockSpec(memory_space=pl.ANY)
AFTER = pl.BlockSpec(memory_space=pltpu.HBM)
SCALARS = pl.BlockSpec(memory_space=pltpu.SMEM)
WHOLE = pl.BlockSpec(memory_space=pltpu.VMEM)
OVER_LAST = (((1,), (1,)), ((), ()))


def halves(x):
    high = x.astype(jnp.bfloat16)
    low = (x - high.astype(jnp.float32)).astype(jnp.bfloat16)
    return high, low


def split_kernel(band_ref, after_ref, out_ref):
    del after_ref
    tile = band_ref.shape[1]
    out_ref[:, pl.ds(0, tile)], out_ref[:, pl.ds(tile, tile)] = halves(band_ref[...])


def split(band, after):
    receivers, depth = band.shape
    tile, rows = min(TILE, depth), receivers // 4
    return pl.pallas_call(
        split_kernel,
        grid=(4, depth // tile),
        in_specs=[pl.BlockSpec((rows, tile), lambda i, j: (i, j)), AFTER],
        out_specs=pl.BlockSpec((rows, 2 * tile), lambda i, j: (i, j)),
        out_shape=jax.ShapeDtypeStruct((receivers, 2 * depth), jnp.bfloat16),
        compiler_params=pltpu.CompilerParams(vmem_limit_bytes=VMEM_LIMIT),
        cost_estimate=pl.CostEstimate(flops=0, bytes_accessed=8 * receivers * depth, transcendentals=0),
        name="band_halves",
    )(band, after)


def multiply(band_ref, slip):
    members = slip.shape[0]
    high, low = halves(slip)
    both = jnp.concatenate([high, low], axis=0)
    mixed = lax.dot_general(
        band_ref[...], jnp.concatenate([both, both], axis=1), OVER_LAST, preferred_element_type=jnp.float32
    )
    return mixed[:, :members] + mixed[:, members:]


def accumulate(total_scr, band_ref, slip):
    step = pl.program_id(0)
    now = multiply(band_ref, slip)

    @pl.when(step == 0)
    def _():
        total_scr[...] = now

    @pl.when(step > 0)
    def _():
        total_scr[...] += now


def in_order(me_ref, ks, slip_refs, slip_scr):
    rows = slip_refs[0].shape[0]
    for k, ref in zip(ks, slip_refs):
        place = pl.multiple_of(((me_ref[0] ^ k) >> 1) * rows, 8)
        slip_scr[pl.ds(place, rows), :] = ref[...]
    return slip_scr[...]


def like_product_kernel(ks, me_ref, band_ref, *refs):
    slip_refs, (after_ref, out_ref, slip_scr) = refs[: len(ks)], refs[len(ks) :]
    del after_ref
    accumulate(out_ref, band_ref, in_order(me_ref, ks, slip_refs, slip_scr))


def part_rows(me_ref, kept_ref, given_ref, parts, crossed):
    pairs, own, _ = kept_ref.shape
    mine = me_ref[0] & 1
    for pair in range(pairs):
        for out_ref, order, parity in ((kept_ref, parts, mine), (given_ref, crossed, 1 - mine)):
            rows = pl.ds(pl.multiple_of((2 * pair + parity) * own, 8), own)
            out_ref[pair] = jnp.concatenate([ref[rows, :] for ref in order], axis=1)


def unlike_product_kernel(ks, me_ref, band_ref, *refs):
    slip_refs, (like_ref, kept_ref, given_ref, slip_scr, total_scr) = refs[: len(ks)], refs[len(ks) :]
    accumulate(total_scr, band_ref, in_order(me_ref, ks, slip_refs, slip_scr))

    @pl.when(pl.program_id(0) == pl.num_programs(0) - 1)
    def _():
        part_rows(me_ref, kept_ref, given_ref, (like_ref, total_scr), (total_scr, like_ref))


def last_product_kernel(me_ref, band_ref, slip_ref, *refs):
    kept_ref, given_ref, total_scr = refs[-3:]
    accumulate(total_scr, band_ref, slip_ref[...])

    @pl.when(pl.program_id(0) == pl.num_programs(0) - 1)
    def _():
        part_rows(me_ref, kept_ref, given_ref, (total_scr,), (total_scr,))


def product(kernel, name, me, band, slip, slip_specs, extra, extra_specs, members, ways, scratch, weight, columns=None):
    receivers, depth = band.shape[0], band.shape[1] // 2
    tile = min(TILE, depth)
    if columns is None:
        shape, many = (receivers, members), 1
    else:
        shape, many = (ways // 2, receivers // ways, columns), 2
    out = pl.BlockSpec(shape, lambda i, me_ref: (0,) * len(shape))
    outs = pl.pallas_call(
        kernel,
        grid_spec=pltpu.PrefetchScalarGridSpec(
            num_scalar_prefetch=1,
            grid=(depth // tile,),
            in_specs=[pl.BlockSpec((receivers, 2 * tile), lambda i, me_ref: (0, i)), *slip_specs, *extra_specs],
            out_specs=[out] * many,
            scratch_shapes=[pltpu.VMEM(rows_columns, jnp.float32) for rows_columns in scratch],
        ),
        out_shape=[jax.ShapeDtypeStruct(shape, jnp.float32)] * many,
        compiler_params=pltpu.CompilerParams(vmem_limit_bytes=VMEM_LIMIT),
        cost_estimate=pl.CostEstimate(
            flops=weight * 8 * receivers * depth * members,
            bytes_accessed=4 * (receivers * depth + members * depth),
            transcendentals=0,
        ),
        name=name,
    )(me, band, *slip, *extra)
    return outs if many == 2 else outs[0]


def first_products(me, band, slip_field, got, ways, after):
    receivers, depth = band.shape[0], band.shape[1] // 2
    tile = min(TILE, depth)
    rows = got[2].shape[0]
    members, steps = ways // 2 * rows, depth // tile
    mine = pl.BlockSpec((rows, tile), lambda i, me_ref: (0, me_ref[0] * steps + i))
    block = pl.BlockSpec((rows, tile), lambda i, me_ref: (0, i))
    even, odd = list(range(0, ways, 2)), list(range(1, ways, 2))
    like = product(
        functools.partial(like_product_kernel, even), "like_product", me, band,
        [slip_field] + [got[k] for k in even[1:]], [mine] + [block] * (len(even) - 1), [after], [AFTER],
        members, ways, [(members, tile)], 1,
    )
    whole = pl.BlockSpec((receivers, members), lambda i, me_ref: (0, 0))
    return like, lambda: product(
        functools.partial(unlike_product_kernel, odd), "unlike_product", me, band,
        [got[k] for k in odd], [block] * len(odd), [like], [whole],
        members, ways, [(members, tile), (receivers, members)], FIRST_WEIGHT, 2 * members,
    )


def last_product(me, band, slip, after, ways):
    receivers, depth = band.shape[0], band.shape[1] // 2
    members = slip.shape[0]
    spec = pl.BlockSpec((members, min(TILE, depth)), lambda i, me_ref: (0, i))
    return product(
        last_product_kernel, "last_product", me, band, [slip], [spec], after, [ANY] * len(after),
        members, ways, [(receivers, members)], 1, members,
    )


def fold_kernel(me_ref, kept_ref, came_ref, *out_refs):
    for k, out_ref in enumerate(out_refs):
        pair = (me_ref[0] >> 1) ^ k
        out_ref[...] = kept_ref[pair] + came_ref[pair]


def last_sums(me, kept, given, ways):
    pairs = ways // 2
    shape = jax.ShapeDtypeStruct(kept.shape[1:], jnp.float32)
    blocks = pl.pallas_call(
        fold_kernel,
        in_specs=[SCALARS, WHOLE, WHOLE],
        out_specs=[WHOLE] * pairs,
        out_shape=[shape] * pairs,
        compiler_params=SMALL,
        name="pair_sums",
    )(me, kept, swap(given, 1, ways))
    return [blocks[0]] + [swap(blocks[k], 2 * k, ways) for k in range(1, pairs)]


def pack_kernel(to_ref, slip_ref, *refs):
    del to_ref
    out_ref = refs[-1]
    out_ref[...] = slip_ref[...]


def pack(to, slip_field, rows, depth, after):
    return pl.pallas_call(
        pack_kernel,
        grid_spec=pltpu.PrefetchScalarGridSpec(
            num_scalar_prefetch=1,
            grid=(1,),
            in_specs=[pl.BlockSpec((rows, depth), lambda i, to_ref: (0, to_ref[0]))] + [AFTER] * len(after),
            out_specs=pl.BlockSpec((rows, depth), lambda i, to_ref: (0, 0)),
        ),
        out_shape=jax.ShapeDtypeStruct((rows, depth), jnp.float32),
        cost_estimate=pl.CostEstimate(flops=0, bytes_accessed=8 * rows * depth, transcendentals=0),
        name="pack_block",
    )(to, slip_field, *after)


def pack_all_kernel(slip_ref, riders_ref, *refs):
    out_ref = refs[-1]
    depth = slip_ref.shape[1]
    out_ref[0, :, pl.ds(0, depth)] = slip_ref[...]
    out_ref[0, :, pl.ds(depth, riders_ref.shape[2])] = riders_ref[0]


def pack_all(slip_field, start, rows, riders, after):
    ways, _, width = riders.shape
    depth = slip_field.shape[1] // ways
    return pl.pallas_call(
        pack_all_kernel,
        grid=(ways,),
        in_specs=[
            pl.BlockSpec((rows, depth), lambda i: (start // rows, i)),
            pl.BlockSpec((1, rows, width), lambda i: (i, 0, 0)),
        ]
        + [AFTER] * len(after),
        out_specs=pl.BlockSpec((1, rows, depth + width), lambda i: (i, 0, 0)),
        out_shape=jax.ShapeDtypeStruct((ways, rows, depth + width), jnp.float32),
        cost_estimate=pl.CostEstimate(flops=0, bytes_accessed=8 * ways * rows * (depth + width), transcendentals=0),
        name="pack_all",
    )(slip_field, riders, *after)


def gather_kernel(elements_ref, slip_ref, after_ref, out_ref, tiles, sems):
    del after_ref
    groups = out_ref.shape[1] // LANES

    def fetch(g):
        def one(j, carry):
            first = pl.multiple_of((elements_ref[g * LANES + j] >> 7) << 7, LANES)
            pltpu.make_async_copy(slip_ref.at[:, pl.ds(first, LANES)], tiles.at[g & 1, j], sems.at[g & 1]).start()
            return carry

        lax.fori_loop(0, LANES, one, 0, unroll=8)

    lanes = lax.broadcasted_iota(jnp.int32, tiles.shape[2:], 1)
    fetch(0)
    for g in range(groups):
        if g + 1 < groups:
            fetch(g + 1)
        slot = tiles.at[g & 1]
        pltpu.make_async_copy(slot, slot, sems.at[g & 1]).wait()

        def one(j, found, g=g, slot=slot):
            shift = (j - elements_ref[g * LANES + j]) & (LANES - 1)
            return jnp.where(lanes == j, pltpu.roll(slot[j], shift, axis=1), found)

        found = lax.fori_loop(0, LANES, one, jnp.zeros(tiles.shape[2:], jnp.float32), unroll=16)
        out_ref[:, pl.ds(g * LANES, LANES)] = found


def gather(elements, slip_field, after):
    members, count = slip_field.shape[0], elements.shape[0]
    return pl.pallas_call(
        gather_kernel,
        in_specs=[SCALARS, ANY, AFTER],
        out_specs=WHOLE,
        out_shape=jax.ShapeDtypeStruct((members, count), jnp.float32),
        scratch_shapes=[pltpu.VMEM((2, LANES, members, LANES), jnp.float32), pltpu.SemaphoreType.DMA((2,))],
        cost_estimate=pl.CostEstimate(flops=0, bytes_accessed=4 * members * LANES * count, transcendentals=0),
        name="slip_at_receivers",
    )(elements, slip_field, after)


def swap(x, bit, ways):
    return lax.ppermute(x, "src", [(i, i ^ bit) for i in range(ways)])


def owner_sums(kept, given, me, ways):
    _, own, columns = kept.shape
    bit = 1
    while True:
        came = swap(given, bit, ways)
        bit *= 2
        if bit >= ways:
            return [kept.reshape(own, columns), came.reshape(own, columns)], given
        pairs = (kept + came).reshape(ways // bit // 2, 2, own, columns)
        mine = (me // bit) & 1
        kept = lax.dynamic_index_in_dim(pairs, mine, 1, keepdims=False)
        given = lax.dynamic_index_in_dim(pairs, 1 - mine, 1, keepdims=False)


def place(count, columns, where):
    shape = (count, columns)
    wanted = where(lax.broadcasted_iota(jnp.int32, shape, 0))
    return jnp.where(lax.broadcasted_iota(jnp.int32, shape, 1) == wanted, 1.0, 0.0).astype(jnp.bfloat16)


def moved(x, places):
    rows = x.shape[0]
    high, rest = halves(x)
    middle = rest.astype(jnp.float32)
    low = (x - high.astype(jnp.float32) - middle).astype(jnp.bfloat16)
    parts = jnp.dot(jnp.concatenate([high, rest, low], axis=0), places, preferred_element_type=jnp.float32)
    return parts[:rows] + (parts[rows : 2 * rows] + parts[2 * rows :])


def upright(row):
    shape = (row.shape[1], row.shape[1])
    diagonal = lax.broadcasted_iota(jnp.int32, shape, 0) == lax.broadcasted_iota(jnp.int32, shape, 1)
    return jnp.sum(jnp.where(diagonal, row, 0.0), axis=1, keepdims=True)


def strength_kernel(static_ref, dynamic_ref, scale_ref, riders_ref, classes_ref, normal_ref, after_ref, out_ref):
    del after_ref
    ways, tail, width = riders_ref.shape
    own, columns = classes_ref.shape
    members = columns // ways
    turned = riders_ref[...].reshape(ways * tail, width).T
    groups = [turned[g * own : (g + 1) * own] for g in range(members // tail)]
    count = ways * tail
    places = place(columns, columns, lambda j: j % count // tail * members + j // count * tail + j % tail)
    slip = moved(jnp.concatenate(groups, axis=1), places)
    classes = classes_ref[...]
    zero = jnp.zeros(classes.shape, jnp.float32)
    mu_static, mu_dynamic, slip_scale = zero, zero, zero
    for index in range(static_ref.shape[0]):
        here = classes == index
        mu_static = jnp.where(here, static_ref[index], mu_static)
        mu_dynamic = jnp.where(here, dynamic_ref[index], mu_dynamic)
        slip_scale = jnp.where(here, scale_ref[index], slip_scale)
    weakening = jnp.maximum(1.0 - jnp.abs(slip) / slip_scale, 0.0)
    out_ref[...] = upright(normal_ref[...]) * (mu_dynamic + (mu_static - mu_dynamic) * weakening)


def strength(came, width, classes, normal, static, dynamic, scale, after):
    ways, tail, total = came.shape
    return pl.pallas_call(
        strength_kernel,
        grid=(1,),
        in_specs=[SCALARS] * 3
        + [pl.BlockSpec((ways, tail, width), lambda i: (0, 0, total // width - 1))]
        + [pl.BlockSpec(classes.shape, lambda i: (0, 0)), pl.BlockSpec((1, normal.shape[0]), lambda i: (0, 0)), ANY],
        out_specs=pl.BlockSpec(classes.shape, lambda i: (0, 0)),
        out_shape=jax.ShapeDtypeStruct(classes.shape, jnp.float32),
        compiler_params=SMALL,
        name="strength",
    )(static, dynamic, scale, came, classes, normal[None, :], after)


def slip_rate_kernel(n_first, load_ref, strength_ref, places_ref, *refs):
    *term_refs, stress_ref, rate_ref = refs
    total = sum(ref[...] for ref in term_refs[n_first:])
    if n_first:
        total = jnp.concatenate([sum(ref[...] for ref in term_refs[:n_first]), total], axis=1)
    stress = upright(load_ref[...]) + moved(total, places_ref[...])
    excess = (stress - strength_ref[...]) / 0.25
    stress_ref[...] = stress
    rate_ref[...] = jnp.maximum(excess, 0.0) + jnp.log1p(jnp.exp(-jnp.abs(excess)))


def slip_rate(load, strong, places, first, last):
    terms = [*first, *last]
    shape = jax.ShapeDtypeStruct(strong.shape, jnp.float32)
    return pl.pallas_call(
        functools.partial(slip_rate_kernel, len(first)),
        in_specs=[WHOLE] * (3 + len(terms)),
        out_specs=[WHOLE] * 2,
        out_shape=[shape, shape],
        compiler_params=SMALL,
        name="slip_rate",
    )(load[None, :], strong, places, *terms)


def partners(ways):
    half, quarter = ways // 2, ways // 4
    order = []
    for parity in (0, 1):
        near = [k for k in [*range(quarter, half), *range(1, quarter)] if k % 2 == parity]
        for far in range(half + parity, ways, 2):
            order.append(far)
            if near:
                order.append(near.pop(0))
    return order


def shards(
    ways,
    kernel_band,
    slip_field,
    elements,
    classes,
    shear_load,
    normal_stress,
    static_friction,
    dynamic_friction,
    weakening_slip,
):
    me = lax.axis_index("src").astype(jnp.int32)
    here = me.reshape(1)
    members, total_elements = slip_field.shape
    depth = total_elements // ways
    own = classes.shape[0]
    tail = min(TAIL_ROWS, members)
    head = members - tail

    came, got, block = [slip_field] * IN_FLIGHT, {}, slip_field
    if head:
        for turn, k in enumerate(partners(ways)):
            block = pack(here ^ k, slip_field, head, depth, (came[-IN_FLIGHT], block))
            got[k] = swap(block, k, ways)
            came.append(got[k])
            if turn == 2:
                came[-1] = at_receivers = gather(elements, slip_field, came[-1])
            if turn == 4:
                came[-1] = band = split(kernel_band, came[-1])
            if turn == 7:
                came[-1], unlike = first_products(here, band, slip_field, got, ways, came[-1])
    else:
        at_receivers = gather(elements, slip_field, slip_field)
        band = split(kernel_band, slip_field)

    riders = at_receivers.reshape(members // tail, tail, ways, own)
    riders = riders.transpose(2, 1, 0, 3).reshape(ways, tail, -1)
    riders = jnp.pad(riders, ((0, 0), (0, 0), (0, -riders.shape[2] % LANES)))
    last = lax.all_to_all(pack_all(slip_field, head, tail, riders, (came[-IN_FLIGHT], block)), "src", 0, 0, tiled=True)

    first_terms, after = [], slip_field
    if head:
        first_terms, after = owner_sums(*unlike(), me, ways)
    places = place(ways * tail, ways * members, lambda j: j // tail * members + head + j % tail)
    if head:
        half = ways // 2 * head
        first_places = place(
            ways * head,
            ways * members,
            lambda j: (j % half // head * 2 + (j // half ^ (me & 1))) * members + j % half % head,
        )
        places = jnp.concatenate([first_places, places], axis=0)
    kept, given = last_product(here, band, last.reshape(ways * tail, -1), (after, places), ways)
    strong = strength(
        last, riders.shape[2], classes, normal_stress, static_friction, dynamic_friction, weakening_slip, given
    )
    return slip_rate(shear_load, strong, places, first_terms, last_sums(here, kept, given, ways))


def solution(mesh):
    placed = (
        P("groups", "src"),
        P(("groups", "src"), None),
        P("groups"),
        P(("groups", "src"), None),
        P(("groups", "src")),
        P(("groups", "src")),
        P(),
        P(),
        P(),
    )
    return jax.shard_map(
        functools.partial(shards, mesh.shape["src"]),
        mesh=mesh,
        in_specs=placed,
        out_specs=(P(("groups", "src"), None), P(("groups", "src"), None)),
        check_vma=False,
    )
```

```python
import functools

import jax
import jax.numpy as jnp
from jax import lax
from jax.experimental import pallas as pl
from jax.experimental.pallas import tpu as pltpu
from jax.sharding import PartitionSpec as P

VMEM_LIMIT = 48 * 1024 * 1024
SMALL = pltpu.CompilerParams(vmem_limit_bytes=8 * 1024 * 1024)
TAIL_ROWS = 8
IN_FLIGHT = 5
TILE = 2048
FIRST_WEIGHT = 10
LANES = 128
ANY = pl.BlockSpec(memory_space=pl.ANY)
AFTER = pl.BlockSpec(memory_space=pltpu.HBM)
SCALARS = pl.BlockSpec(memory_space=pltpu.SMEM)
WHOLE = pl.BlockSpec(memory_space=pltpu.VMEM)
OVER_LAST = (((1,), (1,)), ((), ()))


def halves(x):
    high = x.astype(jnp.bfloat16)
    low = (x - high.astype(jnp.float32)).astype(jnp.bfloat16)
    return high, low


def split_kernel(band_ref, after_ref, out_ref):
    del after_ref
    tile = band_ref.shape[1]
    out_ref[:, pl.ds(0, tile)], out_ref[:, pl.ds(tile, tile)] = halves(band_ref[...])


def split(band, after):
    receivers, depth = band.shape
    tile, rows = min(TILE, depth), receivers // 4
    return pl.pallas_call(
        split_kernel,
        grid=(4, depth // tile),
        in_specs=[pl.BlockSpec((rows, tile), lambda i, j: (i, j)), AFTER],
        out_specs=pl.BlockSpec((rows, 2 * tile), lambda i, j: (i, j)),
        out_shape=jax.ShapeDtypeStruct((receivers, 2 * depth), jnp.bfloat16),
        compiler_params=pltpu.CompilerParams(vmem_limit_bytes=VMEM_LIMIT),
        cost_estimate=pl.CostEstimate(flops=0, bytes_accessed=8 * receivers * depth, transcendentals=0),
        name="band_halves",
    )(band, after)


def multiply(band_ref, slip):
    members = slip.shape[0]
    high, low = halves(slip)
    both = jnp.concatenate([high, low], axis=0)
    mixed = lax.dot_general(
        band_ref[...], jnp.concatenate([both, both], axis=1), OVER_LAST, preferred_element_type=jnp.float32
    )
    return mixed[:, :members] + mixed[:, members:]


def accumulate(total_scr, band_ref, slip):
    step = pl.program_id(0)
    now = multiply(band_ref, slip)

    @pl.when(step == 0)
    def _():
        total_scr[...] = now

    @pl.when(step > 0)
    def _():
        total_scr[...] += now


def in_order(me_ref, ks, slip_refs, slip_scr):
    rows = slip_refs[0].shape[0]
    for k, ref in zip(ks, slip_refs):
        place = pl.multiple_of(((me_ref[0] ^ k) >> 1) * rows, 8)
        slip_scr[pl.ds(place, rows), :] = ref[...]
    return slip_scr[...]


def like_product_kernel(ks, me_ref, band_ref, *refs):
    slip_refs, (after_ref, out_ref, slip_scr) = refs[: len(ks)], refs[len(ks) :]
    del after_ref
    accumulate(out_ref, band_ref, in_order(me_ref, ks, slip_refs, slip_scr))


def part_rows(me_ref, kept_ref, given_ref, parts, crossed):
    pairs, own, _ = kept_ref.shape
    mine = me_ref[0] & 1
    for pair in range(pairs):
        for out_ref, order, parity in ((kept_ref, parts, mine), (given_ref, crossed, 1 - mine)):
            rows = pl.ds(pl.multiple_of((2 * pair + parity) * own, 8), own)
            out_ref[pair] = jnp.concatenate([ref[rows, :] for ref in order], axis=1)


def unlike_product_kernel(ks, me_ref, band_ref, *refs):
    slip_refs, (like_ref, kept_ref, given_ref, slip_scr, total_scr) = refs[: len(ks)], refs[len(ks) :]
    accumulate(total_scr, band_ref, in_order(me_ref, ks, slip_refs, slip_scr))

    @pl.when(pl.program_id(0) == pl.num_programs(0) - 1)
    def _():
        part_rows(me_ref, kept_ref, given_ref, (like_ref, total_scr), (total_scr, like_ref))


def last_product_kernel(me_ref, band_ref, slip_ref, *refs):
    kept_ref, given_ref, total_scr = refs[-3:]
    accumulate(total_scr, band_ref, slip_ref[...])

    @pl.when(pl.program_id(0) == pl.num_programs(0) - 1)
    def _():
        part_rows(me_ref, kept_ref, given_ref, (total_scr,), (total_scr,))


def product(kernel, name, me, band, slip, slip_specs, extra, extra_specs, members, ways, scratch, weight, columns=None):
    receivers, depth = band.shape[0], band.shape[1] // 2
    tile = min(TILE, depth)
    if columns is None:
        shape, many = (receivers, members), 1
    else:
        shape, many = (ways // 2, receivers // ways, columns), 2
    out = pl.BlockSpec(shape, lambda i, me_ref: (0,) * len(shape))
    outs = pl.pallas_call(
        kernel,
        grid_spec=pltpu.PrefetchScalarGridSpec(
            num_scalar_prefetch=1,
            grid=(depth // tile,),
            in_specs=[pl.BlockSpec((receivers, 2 * tile), lambda i, me_ref: (0, i)), *slip_specs, *extra_specs],
            out_specs=[out] * many,
            scratch_shapes=[pltpu.VMEM(rows_columns, jnp.float32) for rows_columns in scratch],
        ),
        out_shape=[jax.ShapeDtypeStruct(shape, jnp.float32)] * many,
        compiler_params=pltpu.CompilerParams(vmem_limit_bytes=VMEM_LIMIT),
        cost_estimate=pl.CostEstimate(
            flops=weight * 8 * receivers * depth * members,
            bytes_accessed=4 * (receivers * depth + members * depth),
            transcendentals=0,
        ),
        name=name,
    )(me, band, *slip, *extra)
    return outs if many == 2 else outs[0]


def first_products(me, band, slip_field, got, ways, after):
    receivers, depth = band.shape[0], band.shape[1] // 2
    tile = min(TILE, depth)
    rows = got[2].shape[0]
    members, steps = ways // 2 * rows, depth // tile
    mine = pl.BlockSpec((rows, tile), lambda i, me_ref: (0, me_ref[0] * steps + i))
    block = pl.BlockSpec((rows, tile), lambda i, me_ref: (0, i))
    even, odd = list(range(0, ways, 2)), list(range(1, ways, 2))
    like = product(
        functools.partial(like_product_kernel, even), "like_product", me, band,
        [slip_field] + [got[k] for k in even[1:]], [mine] + [block] * (len(even) - 1), [after], [AFTER],
        members, ways, [(members, tile)], 1,
    )
    whole = pl.BlockSpec((receivers, members), lambda i, me_ref: (0, 0))
    return like, lambda: product(
        functools.partial(unlike_product_kernel, odd), "unlike_product", me, band,
        [got[k] for k in odd], [block] * len(odd), [like], [whole],
        members, ways, [(members, tile), (receivers, members)], FIRST_WEIGHT, 2 * members,
    )


def last_product(me, band, slip, after, ways):
    receivers, depth = band.shape[0], band.shape[1] // 2
    members = slip.shape[0]
    spec = pl.BlockSpec((members, min(TILE, depth)), lambda i, me_ref: (0, i))
    return product(
        last_product_kernel, "last_product", me, band, [slip], [spec], after, [ANY] * len(after),
        members, ways, [(receivers, members)], 1, members,
    )


def fold_kernel(me_ref, kept_ref, came_ref, *out_refs):
    for k, out_ref in enumerate(out_refs):
        pair = (me_ref[0] >> 1) ^ k
        out_ref[...] = kept_ref[pair] + came_ref[pair]


def last_sums(me, kept, given, ways):
    pairs = ways // 2
    shape = jax.ShapeDtypeStruct(kept.shape[1:], jnp.float32)
    blocks = pl.pallas_call(
        fold_kernel,
        in_specs=[SCALARS, WHOLE, WHOLE],
        out_specs=[WHOLE] * pairs,
        out_shape=[shape] * pairs,
        compiler_params=SMALL,
        name="pair_sums",
    )(me, kept, swap(given, 1, ways))
    return [blocks[0]] + [swap(blocks[k], 2 * k, ways) for k in range(1, pairs)]


def pack_kernel(to_ref, slip_ref, *refs):
    del to_ref
    out_ref = refs[-1]
    out_ref[...] = slip_ref[...]


def pack(to, slip_field, rows, depth, after):
    return pl.pallas_call(
        pack_kernel,
        grid_spec=pltpu.PrefetchScalarGridSpec(
            num_scalar_prefetch=1,
            grid=(1,),
            in_specs=[pl.BlockSpec((rows, depth), lambda i, to_ref: (0, to_ref[0]))] + [AFTER] * len(after),
            out_specs=pl.BlockSpec((rows, depth), lambda i, to_ref: (0, 0)),
        ),
        out_shape=jax.ShapeDtypeStruct((rows, depth), jnp.float32),
        compiler_params=pltpu.CompilerParams(vmem_limit_bytes=VMEM_LIMIT),
        cost_estimate=pl.CostEstimate(flops=0, bytes_accessed=8 * rows * depth, transcendentals=0),
        name="pack_block",
    )(to, slip_field, *after)


def pack_all_kernel(slip_ref, riders_ref, *refs):
    out_ref = refs[-1]
    depth = slip_ref.shape[1]
    out_ref[0, :, pl.ds(0, depth)] = slip_ref[...]
    out_ref[0, :, pl.ds(depth, riders_ref.shape[2])] = riders_ref[0]


def pack_all(slip_field, start, rows, riders, after):
    ways, _, width = riders.shape
    depth = slip_field.shape[1] // ways
    return pl.pallas_call(
        pack_all_kernel,
        grid=(ways,),
        in_specs=[
            pl.BlockSpec((rows, depth), lambda i: (start // rows, i)),
            pl.BlockSpec((1, rows, width), lambda i: (i, 0, 0)),
        ]
        + [AFTER] * len(after),
        out_specs=pl.BlockSpec((1, rows, depth + width), lambda i: (i, 0, 0)),
        out_shape=jax.ShapeDtypeStruct((ways, rows, depth + width), jnp.float32),
        cost_estimate=pl.CostEstimate(flops=0, bytes_accessed=8 * ways * rows * (depth + width), transcendentals=0),
        name="pack_all",
    )(slip_field, riders, *after)


def gather_kernel(elements_ref, slip_ref, after_ref, out_ref, tiles, sems):
    del after_ref
    groups = out_ref.shape[1] // LANES

    def fetch(g):
        def one(j, carry):
            first = pl.multiple_of((elements_ref[g * LANES + j] >> 7) << 7, LANES)
            pltpu.make_async_copy(slip_ref.at[:, pl.ds(first, LANES)], tiles.at[g & 1, j], sems.at[g & 1]).start()
            return carry

        lax.fori_loop(0, LANES, one, 0, unroll=8)

    lanes = lax.broadcasted_iota(jnp.int32, tiles.shape[2:], 1)
    fetch(0)
    for g in range(groups):
        if g + 1 < groups:
            fetch(g + 1)
        slot = tiles.at[g & 1]
        pltpu.make_async_copy(slot, slot, sems.at[g & 1]).wait()

        def one(j, found, g=g, slot=slot):
            shift = (j - elements_ref[g * LANES + j]) & (LANES - 1)
            return jnp.where(lanes == j, pltpu.roll(slot[j], shift, axis=1), found)

        found = lax.fori_loop(0, LANES, one, jnp.zeros(tiles.shape[2:], jnp.float32), unroll=16)
        out_ref[:, pl.ds(g * LANES, LANES)] = found


def gather(elements, slip_field, after):
    members, count = slip_field.shape[0], elements.shape[0]
    return pl.pallas_call(
        gather_kernel,
        in_specs=[SCALARS, ANY, AFTER],
        out_specs=WHOLE,
        out_shape=jax.ShapeDtypeStruct((members, count), jnp.float32),
        scratch_shapes=[pltpu.VMEM((2, LANES, members, LANES), jnp.float32), pltpu.SemaphoreType.DMA((2,))],
        cost_estimate=pl.CostEstimate(flops=0, bytes_accessed=4 * members * LANES * count, transcendentals=0),
        name="slip_at_receivers",
    )(elements, slip_field, after)


def swap(x, bit, ways):
    return lax.ppermute(x, "src", [(i, i ^ bit) for i in range(ways)])


def owner_sums(kept, given, me, ways):
    _, own, columns = kept.shape
    bit = 1
    while True:
        came = swap(given, bit, ways)
        bit *= 2
        if bit >= ways:
            return [kept.reshape(own, columns), came.reshape(own, columns)], given
        pairs = (kept + came).reshape(ways // bit // 2, 2, own, columns)
        mine = (me // bit) & 1
        kept = lax.dynamic_index_in_dim(pairs, mine, 1, keepdims=False)
        given = lax.dynamic_index_in_dim(pairs, 1 - mine, 1, keepdims=False)


def place(count, columns, where):
    shape = (count, columns)
    wanted = where(lax.broadcasted_iota(jnp.int32, shape, 0))
    return jnp.where(lax.broadcasted_iota(jnp.int32, shape, 1) == wanted, 1.0, 0.0).astype(jnp.bfloat16)


def moved(x, places):
    rows = x.shape[0]
    high, rest = halves(x)
    middle = rest.astype(jnp.float32)
    low = (x - high.astype(jnp.float32) - middle).astype(jnp.bfloat16)
    parts = jnp.dot(jnp.concatenate([high, rest, low], axis=0), places, preferred_element_type=jnp.float32)
    return parts[:rows] + (parts[rows : 2 * rows] + parts[2 * rows :])


def upright(row):
    shape = (row.shape[1], row.shape[1])
    diagonal = lax.broadcasted_iota(jnp.int32, shape, 0) == lax.broadcasted_iota(jnp.int32, shape, 1)
    return jnp.sum(jnp.where(diagonal, row, 0.0), axis=1, keepdims=True)


def strength_kernel(static_ref, dynamic_ref, scale_ref, riders_ref, classes_ref, normal_ref, after_ref, out_ref):
    del after_ref
    ways, tail, width = riders_ref.shape
    own, columns = classes_ref.shape
    members = columns // ways
    turned = riders_ref[...].reshape(ways * tail, width).T
    groups = [turned[g * own : (g + 1) * own] for g in range(members // tail)]
    count = ways * tail
    places = place(columns, columns, lambda j: j % count // tail * members + j // count * tail + j % tail)
    slip = moved(jnp.concatenate(groups, axis=1), places)
    classes = classes_ref[...]
    zero = jnp.zeros(classes.shape, jnp.float32)
    mu_static, mu_dynamic, slip_scale = zero, zero, zero
    for index in range(static_ref.shape[0]):
        here = classes == index
        mu_static = jnp.where(here, static_ref[index], mu_static)
        mu_dynamic = jnp.where(here, dynamic_ref[index], mu_dynamic)
        slip_scale = jnp.where(here, scale_ref[index], slip_scale)
    weakening = jnp.maximum(1.0 - jnp.abs(slip) / slip_scale, 0.0)
    out_ref[...] = upright(normal_ref[...]) * (mu_dynamic + (mu_static - mu_dynamic) * weakening)


def strength(came, width, classes, normal, static, dynamic, scale, after):
    ways, tail, total = came.shape
    return pl.pallas_call(
        strength_kernel,
        grid=(1,),
        in_specs=[SCALARS] * 3
        + [pl.BlockSpec((ways, tail, width), lambda i: (0, 0, total // width - 1))]
        + [pl.BlockSpec(classes.shape, lambda i: (0, 0)), pl.BlockSpec((1, normal.shape[0]), lambda i: (0, 0)), ANY],
        out_specs=pl.BlockSpec(classes.shape, lambda i: (0, 0)),
        out_shape=jax.ShapeDtypeStruct(classes.shape, jnp.float32),
        compiler_params=SMALL,
        name="strength",
    )(static, dynamic, scale, came, classes, normal[None, :], after)


def slip_rate_kernel(n_first, load_ref, strength_ref, places_ref, *refs):
    *term_refs, stress_ref, rate_ref = refs
    total = sum(ref[...] for ref in term_refs[n_first:])
    if n_first:
        total = jnp.concatenate([sum(ref[...] for ref in term_refs[:n_first]), total], axis=1)
    stress = upright(load_ref[...]) + moved(total, places_ref[...])
    excess = (stress - strength_ref[...]) / 0.25
    stress_ref[...] = stress
    rate_ref[...] = jnp.maximum(excess, 0.0) + jnp.log1p(jnp.exp(-jnp.abs(excess)))


def slip_rate(load, strong, places, first, last):
    terms = [*first, *last]
    shape = jax.ShapeDtypeStruct(strong.shape, jnp.float32)
    return pl.pallas_call(
        functools.partial(slip_rate_kernel, len(first)),
        in_specs=[WHOLE] * (3 + len(terms)),
        out_specs=[WHOLE] * 2,
        out_shape=[shape, shape],
        compiler_params=SMALL,
        name="slip_rate",
    )(load[None, :], strong, places, *terms)


def partners(ways):
    half, quarter = ways // 2, ways // 4
    order = []
    for parity in (0, 1):
        near = [k for k in [*range(quarter, half), *range(1, quarter)] if k % 2 == parity]
        for far in range(half + parity, ways, 2):
            order.append(far)
            if near:
                order.append(near.pop(0))
    return order


def shards(
    ways,
    kernel_band,
    slip_field,
    elements,
    classes,
    shear_load,
    normal_stress,
    static_friction,
    dynamic_friction,
    weakening_slip,
):
    me = lax.axis_index("src").astype(jnp.int32)
    here = me.reshape(1)
    members, total_elements = slip_field.shape
    depth = total_elements // ways
    own = classes.shape[0]
    tail = min(TAIL_ROWS, members)
    head = members - tail

    came, got, block = [slip_field] * IN_FLIGHT, {}, slip_field
    if head:
        for turn, k in enumerate(partners(ways)):
            block = pack(here ^ k, slip_field, head, depth, (came[-IN_FLIGHT], block))
            got[k] = swap(block, k, ways)
            came.append(got[k])
            if turn == 2:
                came[-1] = at_receivers = gather(elements, slip_field, came[-1])
            if turn == 4:
                came[-1] = band = split(kernel_band, came[-1])
            if turn == 7:
                came[-1], unlike = first_products(here, band, slip_field, got, ways, came[-1])
    else:
        at_receivers = gather(elements, slip_field, slip_field)
        band = split(kernel_band, slip_field)

    riders = at_receivers.reshape(members // tail, tail, ways, own)
    riders = riders.transpose(2, 1, 0, 3).reshape(ways, tail, -1)
    riders = jnp.pad(riders, ((0, 0), (0, 0), (0, -riders.shape[2] % LANES)))
    last = lax.all_to_all(pack_all(slip_field, head, tail, riders, (came[-IN_FLIGHT], block)), "src", 0, 0, tiled=True)

    first_terms, after = [], slip_field
    if head:
        first_terms, after = owner_sums(*unlike(), me, ways)
    places = place(ways * tail, ways * members, lambda j: j // tail * members + head + j % tail)
    if head:
        half = ways // 2 * head
        first_places = place(
            ways * head,
            ways * members,
            lambda j: (j % half // head * 2 + (j // half ^ (me & 1))) * members + j % half % head,
        )
        places = jnp.concatenate([first_places, places], axis=0)
    kept, given = last_product(here, band, last.reshape(ways * tail, -1), (after, places), ways)
    strong = strength(
        last, riders.shape[2], classes, normal_stress, static_friction, dynamic_friction, weakening_slip, given
    )
    return slip_rate(shear_load, strong, places, first_terms, last_sums(here, kept, given, ways))


def solution(mesh):
    placed = (
        P("groups", "src"),
        P(("groups", "src"), None),
        P("groups"),
        P(("groups", "src"), None),
        P(("groups", "src")),
        P(("groups", "src")),
        P(),
        P(),
        P(),
    )
    return jax.shard_map(
        functools.partial(shards, mesh.shape["src"]),
        mesh=mesh,
        in_specs=placed,
        out_specs=(P(("groups", "src"), None), P(("groups", "src"), None)),
        check_vma=False,
    )
```

```python
import functools

import jax
import jax.numpy as jnp
from jax import lax
from jax.experimental import pallas as pl
from jax.experimental.pallas import tpu as pltpu
from jax.sharding import PartitionSpec as P

VMEM_LIMIT = 48 * 1024 * 1024
SMALL = pltpu.CompilerParams(vmem_limit_bytes=8 * 1024 * 1024)
TAIL_ROWS = 8
IN_FLIGHT = 5
TILE = 2048
FIRST_WEIGHT = 10
LANES = 128
ANY = pl.BlockSpec(memory_space=pl.ANY)
AFTER = pl.BlockSpec(memory_space=pltpu.HBM)
SCALARS = pl.BlockSpec(memory_space=pltpu.SMEM)
WHOLE = pl.BlockSpec(memory_space=pltpu.VMEM)
OVER_LAST = (((1,), (1,)), ((), ()))


def halves(x):
    high = x.astype(jnp.bfloat16)
    low = (x - high.astype(jnp.float32)).astype(jnp.bfloat16)
    return high, low


def split_kernel(band_ref, after_ref, out_ref):
    del after_ref
    tile = band_ref.shape[1]
    out_ref[:, pl.ds(0, tile)], out_ref[:, pl.ds(tile, tile)] = halves(band_ref[...])


def split(band, after):
    receivers, depth = band.shape
    tile, rows = min(TILE, depth), receivers // 4
    return pl.pallas_call(
        split_kernel,
        grid=(4, depth // tile),
        in_specs=[pl.BlockSpec((rows, tile), lambda i, j: (i, j)), AFTER],
        out_specs=pl.BlockSpec((rows, 2 * tile), lambda i, j: (i, j)),
        out_shape=jax.ShapeDtypeStruct((receivers, 2 * depth), jnp.bfloat16),
        compiler_params=pltpu.CompilerParams(vmem_limit_bytes=VMEM_LIMIT),
        cost_estimate=pl.CostEstimate(flops=0, bytes_accessed=8 * receivers * depth, transcendentals=0),
        name="band_halves",
    )(band, after)


def multiply(band_ref, slip):
    members = slip.shape[0]
    high, low = halves(slip)
    both = jnp.concatenate([high, low], axis=0)
    mixed = lax.dot_general(
        band_ref[...], jnp.concatenate([both, both], axis=1), OVER_LAST, preferred_element_type=jnp.float32
    )
    return mixed[:, :members] + mixed[:, members:]


def accumulate(total_scr, band_ref, slip):
    step = pl.program_id(0)
    now = multiply(band_ref, slip)

    @pl.when(step == 0)
    def _():
        total_scr[...] = now

    @pl.when(step > 0)
    def _():
        total_scr[...] += now


def in_order(me_ref, ks, slip_refs, slip_scr):
    rows = slip_refs[0].shape[0]
    for k, ref in zip(ks, slip_refs):
        place = pl.multiple_of(((me_ref[0] ^ k) >> 1) * rows, 8)
        slip_scr[pl.ds(place, rows), :] = ref[...]
    return slip_scr[...]


def like_product_kernel(ks, me_ref, band_ref, *refs):
    slip_refs, (after_ref, out_ref, slip_scr) = refs[: len(ks)], refs[len(ks) :]
    del after_ref
    accumulate(out_ref, band_ref, in_order(me_ref, ks, slip_refs, slip_scr))


def part_rows(me_ref, kept_ref, given_ref, parts, crossed):
    pairs, own, _ = kept_ref.shape
    mine = me_ref[0] & 1
    for pair in range(pairs):
        for out_ref, order, parity in ((kept_ref, parts, mine), (given_ref, crossed, 1 - mine)):
            rows = pl.ds(pl.multiple_of((2 * pair + parity) * own, 8), own)
            out_ref[pair] = jnp.concatenate([ref[rows, :] for ref in order], axis=1)


def unlike_product_kernel(ks, me_ref, band_ref, *refs):
    slip_refs, (like_ref, kept_ref, given_ref, slip_scr, total_scr) = refs[: len(ks)], refs[len(ks) :]
    accumulate(total_scr, band_ref, in_order(me_ref, ks, slip_refs, slip_scr))

    @pl.when(pl.program_id(0) == pl.num_programs(0) - 1)
    def _():
        part_rows(me_ref, kept_ref, given_ref, (like_ref, total_scr), (total_scr, like_ref))


def last_product_kernel(me_ref, band_ref, slip_ref, *refs):
    kept_ref, given_ref, total_scr = refs[-3:]
    accumulate(total_scr, band_ref, slip_ref[...])

    @pl.when(pl.program_id(0) == pl.num_programs(0) - 1)
    def _():
        part_rows(me_ref, kept_ref, given_ref, (total_scr,), (total_scr,))


def product(kernel, name, me, band, slip, slip_specs, extra, extra_specs, members, ways, scratch, weight, columns=None):
    receivers, depth = band.shape[0], band.shape[1] // 2
    tile = min(TILE, depth)
    if columns is None:
        shape, many = (receivers, members), 1
    else:
        shape, many = (ways // 2, receivers // ways, columns), 2
    out = pl.BlockSpec(shape, lambda i, me_ref: (0,) * len(shape))
    outs = pl.pallas_call(
        kernel,
        grid_spec=pltpu.PrefetchScalarGridSpec(
            num_scalar_prefetch=1,
            grid=(depth // tile,),
            in_specs=[pl.BlockSpec((receivers, 2 * tile), lambda i, me_ref: (0, i)), *slip_specs, *extra_specs],
            out_specs=[out] * many,
            scratch_shapes=[pltpu.VMEM(rows_columns, jnp.float32) for rows_columns in scratch],
        ),
        out_shape=[jax.ShapeDtypeStruct(shape, jnp.float32)] * many,
        compiler_params=pltpu.CompilerParams(vmem_limit_bytes=VMEM_LIMIT),
        cost_estimate=pl.CostEstimate(
            flops=weight * 8 * receivers * depth * members,
            bytes_accessed=4 * (receivers * depth + members * depth),
            transcendentals=0,
        ),
        name=name,
    )(me, band, *slip, *extra)
    return outs if many == 2 else outs[0]


def first_products(me, band, slip_field, got, ways, after):
    receivers, depth = band.shape[0], band.shape[1] // 2
    tile = min(TILE, depth)
    rows = got[2].shape[0]
    members, steps = ways // 2 * rows, depth // tile
    mine = pl.BlockSpec((rows, tile), lambda i, me_ref: (0, me_ref[0] * steps + i))
    block = pl.BlockSpec((rows, tile), lambda i, me_ref: (0, i))
    even, odd = list(range(0, ways, 2)), list(range(1, ways, 2))
    like = product(
        functools.partial(like_product_kernel, even), "like_product", me, band,
        [slip_field] + [got[k] for k in even[1:]], [mine] + [block] * (len(even) - 1), [after], [AFTER],
        members, ways, [(members, tile)], 1,
    )
    whole = pl.BlockSpec((receivers, members), lambda i, me_ref: (0, 0))
    return like, lambda: product(
        functools.partial(unlike_product_kernel, odd), "unlike_product", me, band,
        [got[k] for k in odd], [block] * len(odd), [like], [whole],
        members, ways, [(members, tile), (receivers, members)], FIRST_WEIGHT, 2 * members,
    )


def last_product(me, band, slip, after, ways):
    receivers, depth = band.shape[0], band.shape[1] // 2
    members = slip.shape[0]
    spec = pl.BlockSpec((members, min(TILE, depth)), lambda i, me_ref: (0, i))
    return product(
        last_product_kernel, "last_product", me, band, [slip], [spec], after, [ANY] * len(after),
        members, ways, [(receivers, members)], 1, members,
    )


def fold_kernel(me_ref, kept_ref, came_ref, *out_refs):
    for k, out_ref in enumerate(out_refs):
        pair = (me_ref[0] >> 1) ^ k
        out_ref[...] = kept_ref[pair] + came_ref[pair]


def last_sums(me, kept, given, ways):
    pairs = ways // 2
    shape = jax.ShapeDtypeStruct(kept.shape[1:], jnp.float32)
    blocks = pl.pallas_call(
        fold_kernel,
        in_specs=[SCALARS, WHOLE, WHOLE],
        out_specs=[WHOLE] * pairs,
        out_shape=[shape] * pairs,
        compiler_params=SMALL,
        name="pair_sums",
    )(me, kept, swap(given, 1, ways))
    return [blocks[0]] + [swap(blocks[k], 2 * k, ways) for k in reversed(range(1, pairs))]


def pack_kernel(to_ref, slip_ref, *refs):
    del to_ref
    out_ref = refs[-1]
    out_ref[...] = slip_ref[...]


def pack(to, slip_field, rows, depth, after):
    return pl.pallas_call(
        pack_kernel,
        grid_spec=pltpu.PrefetchScalarGridSpec(
            num_scalar_prefetch=1,
            grid=(1,),
            in_specs=[pl.BlockSpec((rows, depth), lambda i, to_ref: (0, to_ref[0]))] + [AFTER] * len(after),
            out_specs=pl.BlockSpec((rows, depth), lambda i, to_ref: (0, 0)),
        ),
        out_shape=jax.ShapeDtypeStruct((rows, depth), jnp.float32),
        compiler_params=pltpu.CompilerParams(vmem_limit_bytes=VMEM_LIMIT),
        cost_estimate=pl.CostEstimate(flops=0, bytes_accessed=8 * rows * depth, transcendentals=0),
        name="pack_block",
    )(to, slip_field, *after)


def pack_all_kernel(slip_ref, riders_ref, *refs):
    out_ref = refs[-1]
    depth = slip_ref.shape[1]
    out_ref[0, :, pl.ds(0, depth)] = slip_ref[...]
    out_ref[0, :, pl.ds(depth, riders_ref.shape[2])] = riders_ref[0]


def pack_all(slip_field, start, rows, riders, after):
    ways, _, width = riders.shape
    depth = slip_field.shape[1] // ways
    return pl.pallas_call(
        pack_all_kernel,
        grid=(ways,),
        in_specs=[
            pl.BlockSpec((rows, depth), lambda i: (start // rows, i)),
            pl.BlockSpec((1, rows, width), lambda i: (i, 0, 0)),
        ]
        + [AFTER] * len(after),
        out_specs=pl.BlockSpec((1, rows, depth + width), lambda i: (i, 0, 0)),
        out_shape=jax.ShapeDtypeStruct((ways, rows, depth + width), jnp.float32),
        cost_estimate=pl.CostEstimate(flops=0, bytes_accessed=8 * ways * rows * (depth + width), transcendentals=0),
        name="pack_all",
    )(slip_field, riders, *after)


def gather_kernel(elements_ref, slip_ref, after_ref, out_ref, tiles, sems):
    del after_ref
    groups = out_ref.shape[1] // LANES

    def fetch(g):
        def one(j, carry):
            first = pl.multiple_of((elements_ref[g * LANES + j] >> 7) << 7, LANES)
            pltpu.make_async_copy(slip_ref.at[:, pl.ds(first, LANES)], tiles.at[g & 1, j], sems.at[g & 1]).start()
            return carry

        lax.fori_loop(0, LANES, one, 0, unroll=8)

    lanes = lax.broadcasted_iota(jnp.int32, tiles.shape[2:], 1)
    fetch(0)
    for g in range(groups):
        if g + 1 < groups:
            fetch(g + 1)
        slot = tiles.at[g & 1]
        pltpu.make_async_copy(slot, slot, sems.at[g & 1]).wait()

        def one(j, found, g=g, slot=slot):
            shift = (j - elements_ref[g * LANES + j]) & (LANES - 1)
            return jnp.where(lanes == j, pltpu.roll(slot[j], shift, axis=1), found)

        found = lax.fori_loop(0, LANES, one, jnp.zeros(tiles.shape[2:], jnp.float32), unroll=16)
        out_ref[:, pl.ds(g * LANES, LANES)] = found


def gather(elements, slip_field, after):
    members, count = slip_field.shape[0], elements.shape[0]
    return pl.pallas_call(
        gather_kernel,
        in_specs=[SCALARS, ANY, AFTER],
        out_specs=WHOLE,
        out_shape=jax.ShapeDtypeStruct((members, count), jnp.float32),
        scratch_shapes=[pltpu.VMEM((2, LANES, members, LANES), jnp.float32), pltpu.SemaphoreType.DMA((2,))],
        cost_estimate=pl.CostEstimate(flops=0, bytes_accessed=4 * members * LANES * count, transcendentals=0),
        name="slip_at_receivers",
    )(elements, slip_field, after)


def swap(x, bit, ways):
    return lax.ppermute(x, "src", [(i, i ^ bit) for i in range(ways)])


def owner_sums(kept, given, me, ways):
    _, own, columns = kept.shape
    bit = 1
    while True:
        came = swap(given, bit, ways)
        bit *= 2
        if bit >= ways:
            return [kept.reshape(own, columns), came.reshape(own, columns)], given
        pairs = (kept + came).reshape(ways // bit // 2, 2, own, columns)
        mine = (me // bit) & 1
        kept = lax.dynamic_index_in_dim(pairs, mine, 1, keepdims=False)
        given = lax.dynamic_index_in_dim(pairs, 1 - mine, 1, keepdims=False)


def place(count, columns, where):
    shape = (count, columns)
    wanted = where(lax.broadcasted_iota(jnp.int32, shape, 0))
    return jnp.where(lax.broadcasted_iota(jnp.int32, shape, 1) == wanted, 1.0, 0.0).astype(jnp.bfloat16)


def moved(x, places):
    rows = x.shape[0]
    high, rest = halves(x)
    middle = rest.astype(jnp.float32)
    low = (x - high.astype(jnp.float32) - middle).astype(jnp.bfloat16)
    parts = jnp.dot(jnp.concatenate([high, rest, low], axis=0), places, preferred_element_type=jnp.float32)
    return parts[:rows] + (parts[rows : 2 * rows] + parts[2 * rows :])


def upright(row):
    shape = (row.shape[1], row.shape[1])
    diagonal = lax.broadcasted_iota(jnp.int32, shape, 0) == lax.broadcasted_iota(jnp.int32, shape, 1)
    return jnp.sum(jnp.where(diagonal, row, 0.0), axis=1, keepdims=True)


def strength_kernel(static_ref, dynamic_ref, scale_ref, riders_ref, classes_ref, normal_ref, after_ref, out_ref):
    del after_ref
    ways, tail, width = riders_ref.shape
    own, columns = classes_ref.shape
    members = columns // ways
    turned = riders_ref[...].reshape(ways * tail, width).T
    groups = [turned[g * own : (g + 1) * own] for g in range(members // tail)]
    count = ways * tail
    places = place(columns, columns, lambda j: j % count // tail * members + j // count * tail + j % tail)
    slip = moved(jnp.concatenate(groups, axis=1), places)
    classes = classes_ref[...]
    zero = jnp.zeros(classes.shape, jnp.float32)
    mu_static, mu_dynamic, slip_scale = zero, zero, zero
    for index in range(static_ref.shape[0]):
        here = classes == index
        mu_static = jnp.where(here, static_ref[index], mu_static)
        mu_dynamic = jnp.where(here, dynamic_ref[index], mu_dynamic)
        slip_scale = jnp.where(here, scale_ref[index], slip_scale)
    weakening = jnp.maximum(1.0 - jnp.abs(slip) / slip_scale, 0.0)
    out_ref[...] = upright(normal_ref[...]) * (mu_dynamic + (mu_static - mu_dynamic) * weakening)


def strength(came, width, classes, normal, static, dynamic, scale, after):
    ways, tail, total = came.shape
    return pl.pallas_call(
        strength_kernel,
        grid=(1,),
        in_specs=[SCALARS] * 3
        + [pl.BlockSpec((ways, tail, width), lambda i: (0, 0, total // width - 1))]
        + [pl.BlockSpec(classes.shape, lambda i: (0, 0)), pl.BlockSpec((1, normal.shape[0]), lambda i: (0, 0)), ANY],
        out_specs=pl.BlockSpec(classes.shape, lambda i: (0, 0)),
        out_shape=jax.ShapeDtypeStruct(classes.shape, jnp.float32),
        compiler_params=SMALL,
        name="strength",
    )(static, dynamic, scale, came, classes, normal[None, :], after)


def slip_rate_kernel(n_first, load_ref, strength_ref, places_ref, *refs):
    *term_refs, stress_ref, rate_ref = refs
    total = sum(ref[...] for ref in term_refs[n_first:])
    if n_first:
        total = jnp.concatenate([sum(ref[...] for ref in term_refs[:n_first]), total], axis=1)
    stress = upright(load_ref[...]) + moved(total, places_ref[...])
    excess = (stress - strength_ref[...]) / 0.25
    stress_ref[...] = stress
    rate_ref[...] = jnp.maximum(excess, 0.0) + jnp.log1p(jnp.exp(-jnp.abs(excess)))


def slip_rate(load, strong, places, first, last):
    terms = [*first, *last]
    shape = jax.ShapeDtypeStruct(strong.shape, jnp.float32)
    return pl.pallas_call(
        functools.partial(slip_rate_kernel, len(first)),
        in_specs=[WHOLE] * (3 + len(terms)),
        out_specs=[WHOLE] * 2,
        out_shape=[shape, shape],
        compiler_params=SMALL,
        name="slip_rate",
    )(load[None, :], strong, places, *terms)


def partners(ways):
    half, quarter = ways // 2, ways // 4
    order = []
    for parity in (0, 1):
        near = [k for k in [*range(quarter, half), *range(1, quarter)] if k % 2 == parity]
        for far in range(half + parity, ways, 2):
            order.append(far)
            if near:
                order.append(near.pop(0))
    return order


def shards(
    ways,
    kernel_band,
    slip_field,
    elements,
    classes,
    shear_load,
    normal_stress,
    static_friction,
    dynamic_friction,
    weakening_slip,
):
    me = lax.axis_index("src").astype(jnp.int32)
    here = me.reshape(1)
    members, total_elements = slip_field.shape
    depth = total_elements // ways
    own = classes.shape[0]
    tail = min(TAIL_ROWS, members)
    head = members - tail

    came, got, block = [slip_field] * IN_FLIGHT, {}, slip_field
    if head:
        for turn, k in enumerate(partners(ways)):
            block = pack(here ^ k, slip_field, head, depth, (came[-IN_FLIGHT], block))
            got[k] = swap(block, k, ways)
            came.append(got[k])
            if turn == 2:
                came[-1] = at_receivers = gather(elements, slip_field, came[-1])
            if turn == 4:
                came[-1] = band = split(kernel_band, came[-1])
            if turn == 7:
                came[-1], unlike = first_products(here, band, slip_field, got, ways, came[-1])
    else:
        at_receivers = gather(elements, slip_field, slip_field)
        band = split(kernel_band, slip_field)

    riders = at_receivers.reshape(members // tail, tail, ways, own)
    riders = riders.transpose(2, 1, 0, 3).reshape(ways, tail, -1)
    riders = jnp.pad(riders, ((0, 0), (0, 0), (0, -riders.shape[2] % LANES)))
    last = lax.all_to_all(pack_all(slip_field, head, tail, riders, (came[-IN_FLIGHT], block)), "src", 0, 0, tiled=True)

    first_terms, after = [], slip_field
    if head:
        first_terms, after = owner_sums(*unlike(), me, ways)
    places = place(ways * tail, ways * members, lambda j: j // tail * members + head + j % tail)
    if head:
        half = ways // 2 * head
        first_places = place(
            ways * head,
            ways * members,
            lambda j: (j % half // head * 2 + (j // half ^ (me & 1))) * members + j % half % head,
        )
        places = jnp.concatenate([first_places, places], axis=0)
    kept, given = last_product(here, band, last.reshape(ways * tail, -1), (after, places), ways)
    strong = strength(
        last, riders.shape[2], classes, normal_stress, static_friction, dynamic_friction, weakening_slip, given
    )
    return slip_rate(shear_load, strong, places, first_terms, last_sums(here, kept, given, ways))


def solution(mesh):
    placed = (
        P("groups", "src"),
        P(("groups", "src"), None),
        P("groups"),
        P(("groups", "src"), None),
        P(("groups", "src")),
        P(("groups", "src")),
        P(),
        P(),
        P(),
    )
    return jax.shard_map(
        functools.partial(shards, mesh.shape["src"]),
        mesh=mesh,
        in_specs=placed,
        out_specs=(P(("groups", "src"), None), P(("groups", "src"), None)),
        check_vma=False,
    )
```

```python
import functools

import jax
import jax.numpy as jnp
from jax import lax
from jax.experimental import pallas as pl
from jax.experimental.pallas import tpu as pltpu
from jax.sharding import PartitionSpec as P

VMEM_LIMIT = 48 * 1024 * 1024
SMALL = pltpu.CompilerParams(vmem_limit_bytes=8 * 1024 * 1024)
TAIL_ROWS = 8
IN_FLIGHT = 5
TILE = 2048
FIRST_WEIGHT = 10
LANES = 128
ANY = pl.BlockSpec(memory_space=pl.ANY)
AFTER = pl.BlockSpec(memory_space=pltpu.HBM)
SCALARS = pl.BlockSpec(memory_space=pltpu.SMEM)
WHOLE = pl.BlockSpec(memory_space=pltpu.VMEM)
OVER_LAST = (((1,), (1,)), ((), ()))


def halves(x):
    high = x.astype(jnp.bfloat16)
    low = (x - high.astype(jnp.float32)).astype(jnp.bfloat16)
    return high, low


def split_kernel(band_ref, after_ref, out_ref):
    del after_ref
    tile = band_ref.shape[1]
    out_ref[:, pl.ds(0, tile)], out_ref[:, pl.ds(tile, tile)] = halves(band_ref[...])


def split(band, after):
    receivers, depth = band.shape
    tile, rows = min(TILE, depth), receivers // 4
    return pl.pallas_call(
        split_kernel,
        grid=(4, depth // tile),
        in_specs=[pl.BlockSpec((rows, tile), lambda i, j: (i, j)), AFTER],
        out_specs=pl.BlockSpec((rows, 2 * tile), lambda i, j: (i, j)),
        out_shape=jax.ShapeDtypeStruct((receivers, 2 * depth), jnp.bfloat16),
        compiler_params=pltpu.CompilerParams(vmem_limit_bytes=VMEM_LIMIT),
        cost_estimate=pl.CostEstimate(flops=0, bytes_accessed=8 * receivers * depth, transcendentals=0),
        name="band_halves",
    )(band, after)


def multiply(band_ref, slip):
    members = slip.shape[0]
    high, low = halves(slip)
    both = jnp.concatenate([high, low], axis=0)
    mixed = lax.dot_general(
        band_ref[...], jnp.concatenate([both, both], axis=1), OVER_LAST, preferred_element_type=jnp.float32
    )
    return mixed[:, :members] + mixed[:, members:]


def accumulate(total_scr, band_ref, slip):
    step = pl.program_id(0)
    now = multiply(band_ref, slip)

    @pl.when(step == 0)
    def _():
        total_scr[...] = now

    @pl.when(step > 0)
    def _():
        total_scr[...] += now


def in_order(me_ref, ks, slip_refs, slip_scr):
    rows = slip_refs[0].shape[0]
    for k, ref in zip(ks, slip_refs):
        place = pl.multiple_of(((me_ref[0] ^ k) >> 1) * rows, 8)
        slip_scr[pl.ds(place, rows), :] = ref[...]
    return slip_scr[...]


def like_product_kernel(ks, me_ref, band_ref, *refs):
    slip_refs, (after_ref, out_ref, slip_scr) = refs[: len(ks)], refs[len(ks) :]
    del after_ref
    accumulate(out_ref, band_ref, in_order(me_ref, ks, slip_refs, slip_scr))


def part_rows(me_ref, kept_ref, given_ref, parts, crossed):
    pairs, own, _ = kept_ref.shape
    mine = me_ref[0] & 1
    for pair in range(pairs):
        for out_ref, order, parity in ((kept_ref, parts, mine), (given_ref, crossed, 1 - mine)):
            rows = pl.ds(pl.multiple_of((2 * pair + parity) * own, 8), own)
            out_ref[pair] = jnp.concatenate([ref[rows, :] for ref in order], axis=1)


def unlike_product_kernel(ks, me_ref, band_ref, *refs):
    slip_refs, (like_ref, kept_ref, given_ref, slip_scr, total_scr) = refs[: len(ks)], refs[len(ks) :]
    accumulate(total_scr, band_ref, in_order(me_ref, ks, slip_refs, slip_scr))

    @pl.when(pl.program_id(0) == pl.num_programs(0) - 1)
    def _():
        part_rows(me_ref, kept_ref, given_ref, (like_ref, total_scr), (total_scr, like_ref))


def last_product_kernel(me_ref, band_ref, slip_ref, *refs):
    kept_ref, given_ref, total_scr = refs[-3:]
    accumulate(total_scr, band_ref, slip_ref[...])

    @pl.when(pl.program_id(0) == pl.num_programs(0) - 1)
    def _():
        part_rows(me_ref, kept_ref, given_ref, (total_scr,), (total_scr,))


def product(kernel, name, me, band, slip, slip_specs, extra, extra_specs, members, ways, scratch, weight, columns=None):
    receivers, depth = band.shape[0], band.shape[1] // 2
    tile = min(TILE, depth)
    if columns is None:
        shape, many = (receivers, members), 1
    else:
        shape, many = (ways // 2, receivers // ways, columns), 2
    out = pl.BlockSpec(shape, lambda i, me_ref: (0,) * len(shape))
    outs = pl.pallas_call(
        kernel,
        grid_spec=pltpu.PrefetchScalarGridSpec(
            num_scalar_prefetch=1,
            grid=(depth // tile,),
            in_specs=[pl.BlockSpec((receivers, 2 * tile), lambda i, me_ref: (0, i)), *slip_specs, *extra_specs],
            out_specs=[out] * many,
            scratch_shapes=[pltpu.VMEM(rows_columns, jnp.float32) for rows_columns in scratch],
        ),
        out_shape=[jax.ShapeDtypeStruct(shape, jnp.float32)] * many,
        compiler_params=pltpu.CompilerParams(vmem_limit_bytes=VMEM_LIMIT),
        cost_estimate=pl.CostEstimate(
            flops=weight * 8 * receivers * depth * members,
            bytes_accessed=4 * (receivers * depth + members * depth),
            transcendentals=0,
        ),
        name=name,
    )(me, band, *slip, *extra)
    return outs if many == 2 else outs[0]


def first_products(me, band, slip_field, got, ways, after):
    receivers, depth = band.shape[0], band.shape[1] // 2
    tile = min(TILE, depth)
    rows = got[2].shape[0]
    members, steps = ways // 2 * rows, depth // tile
    mine = pl.BlockSpec((rows, tile), lambda i, me_ref: (0, me_ref[0] * steps + i))
    block = pl.BlockSpec((rows, tile), lambda i, me_ref: (0, i))
    even, odd = list(range(0, ways, 2)), list(range(1, ways, 2))
    like = product(
        functools.partial(like_product_kernel, even), "like_product", me, band,
        [slip_field] + [got[k] for k in even[1:]], [mine] + [block] * (len(even) - 1), [after], [AFTER],
        members, ways, [(members, tile)], 1,
    )
    whole = pl.BlockSpec((receivers, members), lambda i, me_ref: (0, 0))
    return like, lambda: product(
        functools.partial(unlike_product_kernel, odd), "unlike_product", me, band,
        [got[k] for k in odd], [block] * len(odd), [like], [whole],
        members, ways, [(members, tile), (receivers, members)], FIRST_WEIGHT, 2 * members,
    )


def last_product(me, band, slip, after, ways):
    receivers, depth = band.shape[0], band.shape[1] // 2
    members = slip.shape[0]
    spec = pl.BlockSpec((members, min(TILE, depth)), lambda i, me_ref: (0, i))
    return product(
        last_product_kernel, "last_product", me, band, [slip], [spec], after, [ANY] * len(after),
        members, ways, [(receivers, members)], 1, members,
    )


def fold_kernel(me_ref, kept_ref, came_ref, after_ref, *out_refs):
    del after_ref
    for k, out_ref in enumerate(out_refs):
        pair = (me_ref[0] >> 1) ^ k
        out_ref[...] = kept_ref[pair] + came_ref[pair]


def last_sums(me, kept, given, after, ways):
    pairs = ways // 2
    shape = jax.ShapeDtypeStruct(kept.shape[1:], jnp.float32)
    blocks = pl.pallas_call(
        fold_kernel,
        in_specs=[SCALARS, WHOLE, WHOLE, ANY],
        out_specs=[WHOLE] * pairs,
        out_shape=[shape] * pairs,
        compiler_params=SMALL,
        name="pair_sums",
    )(me, kept, swap(given, 1, ways), after)
    return [blocks[0]] + [swap(blocks[k], 2 * k, ways) for k in reversed(range(1, pairs))]


def pack_kernel(to_ref, slip_ref, *refs):
    del to_ref
    out_ref = refs[-1]
    out_ref[...] = slip_ref[...]


def pack(to, slip_field, rows, depth, after):
    return pl.pallas_call(
        pack_kernel,
        grid_spec=pltpu.PrefetchScalarGridSpec(
            num_scalar_prefetch=1,
            grid=(1,),
            in_specs=[pl.BlockSpec((rows, depth), lambda i, to_ref: (0, to_ref[0]))] + [AFTER] * len(after),
            out_specs=pl.BlockSpec((rows, depth), lambda i, to_ref: (0, 0)),
        ),
        out_shape=jax.ShapeDtypeStruct((rows, depth), jnp.float32),
        compiler_params=pltpu.CompilerParams(vmem_limit_bytes=VMEM_LIMIT),
        cost_estimate=pl.CostEstimate(flops=0, bytes_accessed=8 * rows * depth, transcendentals=0),
        name="pack_block",
    )(to, slip_field, *after)


def pack_all_kernel(slip_ref, riders_ref, *refs):
    out_ref = refs[-1]
    depth = slip_ref.shape[1]
    out_ref[0, :, pl.ds(0, depth)] = slip_ref[...]
    out_ref[0, :, pl.ds(depth, riders_ref.shape[2])] = riders_ref[0]


def pack_all(slip_field, start, rows, riders, after):
    ways, _, width = riders.shape
    depth = slip_field.shape[1] // ways
    return pl.pallas_call(
        pack_all_kernel,
        grid=(ways,),
        in_specs=[
            pl.BlockSpec((rows, depth), lambda i: (start // rows, i)),
            pl.BlockSpec((1, rows, width), lambda i: (i, 0, 0)),
        ]
        + [AFTER] * len(after),
        out_specs=pl.BlockSpec((1, rows, depth + width), lambda i: (i, 0, 0)),
        out_shape=jax.ShapeDtypeStruct((ways, rows, depth + width), jnp.float32),
        cost_estimate=pl.CostEstimate(flops=0, bytes_accessed=8 * ways * rows * (depth + width), transcendentals=0),
        name="pack_all",
    )(slip_field, riders, *after)


def gather_kernel(elements_ref, slip_ref, after_ref, out_ref, tiles, sems):
    del after_ref
    groups = out_ref.shape[1] // LANES

    def fetch(g):
        def one(j, carry):
            first = pl.multiple_of((elements_ref[g * LANES + j] >> 7) << 7, LANES)
            pltpu.make_async_copy(slip_ref.at[:, pl.ds(first, LANES)], tiles.at[g & 1, j], sems.at[g & 1]).start()
            return carry

        lax.fori_loop(0, LANES, one, 0, unroll=8)

    lanes = lax.broadcasted_iota(jnp.int32, tiles.shape[2:], 1)
    fetch(0)
    for g in range(groups):
        if g + 1 < groups:
            fetch(g + 1)
        slot = tiles.at[g & 1]
        pltpu.make_async_copy(slot, slot, sems.at[g & 1]).wait()

        def one(j, found, g=g, slot=slot):
            shift = (j - elements_ref[g * LANES + j]) & (LANES - 1)
            return jnp.where(lanes == j, pltpu.roll(slot[j], shift, axis=1), found)

        found = lax.fori_loop(0, LANES, one, jnp.zeros(tiles.shape[2:], jnp.float32), unroll=16)
        out_ref[:, pl.ds(g * LANES, LANES)] = found


def gather(elements, slip_field, after):
    members, count = slip_field.shape[0], elements.shape[0]
    return pl.pallas_call(
        gather_kernel,
        in_specs=[SCALARS, ANY, AFTER],
        out_specs=WHOLE,
        out_shape=jax.ShapeDtypeStruct((members, count), jnp.float32),
        scratch_shapes=[pltpu.VMEM((2, LANES, members, LANES), jnp.float32), pltpu.SemaphoreType.DMA((2,))],
        cost_estimate=pl.CostEstimate(flops=0, bytes_accessed=4 * members * LANES * count, transcendentals=0),
        name="slip_at_receivers",
    )(elements, slip_field, after)


def swap(x, bit, ways):
    return lax.ppermute(x, "src", [(i, i ^ bit) for i in range(ways)])


def owner_sums(kept, given, me, ways):
    _, own, columns = kept.shape
    bit = 1
    while True:
        came = swap(given, bit, ways)
        bit *= 2
        if bit >= ways:
            return [kept.reshape(own, columns), came.reshape(own, columns)], given
        pairs = (kept + came).reshape(ways // bit // 2, 2, own, columns)
        mine = (me // bit) & 1
        kept = lax.dynamic_index_in_dim(pairs, mine, 1, keepdims=False)
        given = lax.dynamic_index_in_dim(pairs, 1 - mine, 1, keepdims=False)


def place(count, columns, where):
    shape = (count, columns)
    wanted = where(lax.broadcasted_iota(jnp.int32, shape, 0))
    return jnp.where(lax.broadcasted_iota(jnp.int32, shape, 1) == wanted, 1.0, 0.0).astype(jnp.bfloat16)


def moved(x, places):
    rows = x.shape[0]
    high, rest = halves(x)
    middle = rest.astype(jnp.float32)
    low = (x - high.astype(jnp.float32) - middle).astype(jnp.bfloat16)
    parts = jnp.dot(jnp.concatenate([high, rest, low], axis=0), places, preferred_element_type=jnp.float32)
    return parts[:rows] + (parts[rows : 2 * rows] + parts[2 * rows :])


def upright(row):
    shape = (row.shape[1], row.shape[1])
    diagonal = lax.broadcasted_iota(jnp.int32, shape, 0) == lax.broadcasted_iota(jnp.int32, shape, 1)
    return jnp.sum(jnp.where(diagonal, row, 0.0), axis=1, keepdims=True)


def strength_kernel(static_ref, dynamic_ref, scale_ref, riders_ref, classes_ref, normal_ref, after_ref, out_ref):
    del after_ref
    ways, tail, width = riders_ref.shape
    own, columns = classes_ref.shape
    members = columns // ways
    turned = riders_ref[...].reshape(ways * tail, width).T
    groups = [turned[g * own : (g + 1) * own] for g in range(members // tail)]
    count = ways * tail
    places = place(columns, columns, lambda j: j % count // tail * members + j // count * tail + j % tail)
    slip = moved(jnp.concatenate(groups, axis=1), places)
    classes = classes_ref[...]
    zero = jnp.zeros(classes.shape, jnp.float32)
    mu_static, mu_dynamic, slip_scale = zero, zero, zero
    for index in range(static_ref.shape[0]):
        here = classes == index
        mu_static = jnp.where(here, static_ref[index], mu_static)
        mu_dynamic = jnp.where(here, dynamic_ref[index], mu_dynamic)
        slip_scale = jnp.where(here, scale_ref[index], slip_scale)
    weakening = jnp.maximum(1.0 - jnp.abs(slip) / slip_scale, 0.0)
    out_ref[...] = upright(normal_ref[...]) * (mu_dynamic + (mu_static - mu_dynamic) * weakening)


def strength(came, width, classes, normal, static, dynamic, scale, after):
    ways, tail, total = came.shape
    return pl.pallas_call(
        strength_kernel,
        grid=(1,),
        in_specs=[SCALARS] * 3
        + [pl.BlockSpec((ways, tail, width), lambda i: (0, 0, total // width - 1))]
        + [pl.BlockSpec(classes.shape, lambda i: (0, 0)), pl.BlockSpec((1, normal.shape[0]), lambda i: (0, 0)), ANY],
        out_specs=pl.BlockSpec(classes.shape, lambda i: (0, 0)),
        out_shape=jax.ShapeDtypeStruct(classes.shape, jnp.float32),
        compiler_params=SMALL,
        name="strength",
    )(static, dynamic, scale, came, classes, normal[None, :], after)


def slip_rate_kernel(n_first, load_ref, strength_ref, places_ref, *refs):
    *term_refs, stress_ref, rate_ref = refs
    total = sum(ref[...] for ref in term_refs[n_first:])
    if n_first:
        total = jnp.concatenate([sum(ref[...] for ref in term_refs[:n_first]), total], axis=1)
    stress = upright(load_ref[...]) + moved(total, places_ref[...])
    excess = (stress - strength_ref[...]) / 0.25
    stress_ref[...] = stress
    rate_ref[...] = jnp.maximum(excess, 0.0) + jnp.log1p(jnp.exp(-jnp.abs(excess)))


def slip_rate(load, strong, places, first, last):
    terms = [*first, *last]
    shape = jax.ShapeDtypeStruct(strong.shape, jnp.float32)
    return pl.pallas_call(
        functools.partial(slip_rate_kernel, len(first)),
        in_specs=[WHOLE] * (3 + len(terms)),
        out_specs=[WHOLE] * 2,
        out_shape=[shape, shape],
        compiler_params=SMALL,
        name="slip_rate",
    )(load[None, :], strong, places, *terms)


def partners(ways):
    half, quarter = ways // 2, ways // 4
    order = []
    for parity in (0, 1):
        near = [k for k in [*range(quarter, half), *range(1, quarter)] if k % 2 == parity]
        for far in range(half + parity, ways, 2):
            order.append(far)
            if near:
                order.append(near.pop(0))
    return order


def shards(
    ways,
    kernel_band,
    slip_field,
    elements,
    classes,
    shear_load,
    normal_stress,
    static_friction,
    dynamic_friction,
    weakening_slip,
):
    me = lax.axis_index("src").astype(jnp.int32)
    here = me.reshape(1)
    members, total_elements = slip_field.shape
    depth = total_elements // ways
    own = classes.shape[0]
    tail = min(TAIL_ROWS, members)
    head = members - tail

    came, got, block = [slip_field] * IN_FLIGHT, {}, slip_field
    if head:
        for turn, k in enumerate(partners(ways)):
            block = pack(here ^ k, slip_field, head, depth, (came[-IN_FLIGHT], block))
            got[k] = swap(block, k, ways)
            came.append(got[k])
            if turn == 2:
                came[-1] = at_receivers = gather(elements, slip_field, came[-1])
            if turn == 4:
                came[-1] = band = split(kernel_band, came[-1])
            if turn == 7:
                came[-1], unlike = first_products(here, band, slip_field, got, ways, came[-1])
    else:
        at_receivers = gather(elements, slip_field, slip_field)
        band = split(kernel_band, slip_field)

    riders = at_receivers.reshape(members // tail, tail, ways, own)
    riders = riders.transpose(2, 1, 0, 3).reshape(ways, tail, -1)
    riders = jnp.pad(riders, ((0, 0), (0, 0), (0, -riders.shape[2] % LANES)))
    last = lax.all_to_all(pack_all(slip_field, head, tail, riders, (came[-IN_FLIGHT], block)), "src", 0, 0, tiled=True)

    first_terms, after = [], slip_field
    if head:
        first_terms, after = owner_sums(*unlike(), me, ways)
    places = place(ways * tail, ways * members, lambda j: j // tail * members + head + j % tail)
    if head:
        half = ways // 2 * head
        first_places = place(
            ways * head,
            ways * members,
            lambda j: (j % half // head * 2 + (j // half ^ (me & 1))) * members + j % half % head,
        )
        places = jnp.concatenate([first_places, places], axis=0)
    kept, given = last_product(here, band, last.reshape(ways * tail, -1), (after, places), ways)
    strong = strength(
        last, riders.shape[2], classes, normal_stress, static_friction, dynamic_friction, weakening_slip, given
    )
    return slip_rate(shear_load, strong, places, first_terms, last_sums(here, kept, given, strong, ways))


def solution(mesh):
    placed = (
        P("groups", "src"),
        P(("groups", "src"), None),
        P("groups"),
        P(("groups", "src"), None),
        P(("groups", "src")),
        P(("groups", "src")),
        P(),
        P(),
        P(),
    )
    return jax.shard_map(
        functools.partial(shards, mesh.shape["src"]),
        mesh=mesh,
        in_specs=placed,
        out_specs=(P(("groups", "src"), None), P(("groups", "src"), None)),
        check_vma=False,
    )
```
